32 devices in a mesh: groups: 2 (over y), expert: 8 (over z, x), hidden: 2 (over core).
Axes of the slice: x: 2, y: 2, z: 4, core: 2. Of those that a mesh axis runs over, the one named last changes fastest.
Arguments:
- current: bfloat16 [2048, 2048], P(('groups', 'expert'), 'hidden'), parts along dimension 0, may hold values from -6 to 6
- previous: float32 [2048, 2048], P(('groups', 'expert'), 'hidden'), parts along dimension 0, may hold values from -6 to 6
- expert_ids: int32 [2048, 8], P(('groups', 'expert')), parts along dimension 0, may hold values from 0 to 15, all different within a row; in each aligned block of 128 rows (0 to 127, 128 to 255, ...) at most 72 rows name the same one
- gate_values: float32 [2048, 8], P(('groups', 'expert')), parts along dimension 0, may hold values from 0.1 to 1
- norm_gain: float32 [2048], replicated, may hold values from 0.1 to 1.9
- expert_gate: bfloat16 [16, 2048, 768], P('expert', 'hidden'), may hold values from -0.125 to 0.125
- expert_up: bfloat16 [16, 2048, 768], P('expert', 'hidden'), may hold values from -0.125 to 0.125
- expert_down: bfloat16 [16, 768, 2048], P('expert', None, 'hidden'), may hold values from -0.21875 to 0.21875
- dense_gate: bfloat16 [2048, 3072], P('expert', 'hidden'), may hold values from -0.125 to 0.125
- dense_up: bfloat16 [2048, 3072], P('expert', 'hidden'), may hold values from -0.125 to 0.125
- dense_down: bfloat16 [3072, 2048], P('hidden', 'expert'), may hold values from -0.109375 to 0.109375
Outputs:
- layer_out: bfloat16 [2048, 2048], P(('groups', 'expert'), 'hidden'), parts along dimension 0
The draws below stay inside these ranges and needn't reach their ends.
There are 2 independent parts, one for each index of `groups`. The reference program is written for one: setup_inputs(seed, part) draws one part's arguments, and reference() takes and returns one part's arrays. A program takes and returns all parts, laid end to end along the dimension named above; an argument that names none is the same for every part. Nothing has to cross between parts.
Inputs may be any that keep to these rules, and one draw needn't show every extreme that they name: `expert_ids`: each row names 8 different experts. Within the rows of one index of the expert axis (aligned blocks of 128 rows) no expert is named by more than 72 rows, and in every draw some expert is named by exactly 72 rows of some block.
All inputs are finite; a program needn't handle non-finite values.
Results may differ from the reference program's by a relative error of at most 0.02.
Values may be sent and summed in bfloat16 or wider, within the bound.
A program may use at most 64 MiB of HBM per device.

```python
import math
import jax
import jax.numpy as jnp
import numpy as np
from jax import lax

D = 2048
F = 768
FFD = 3072
TOP_K = 8
TOK_DEV = 128
EXPERTS = 16
TOKENS = 1024
CAP = 72
N_EXPERT = 8
N_HIDDEN = 2


def shard_levels(own_key, shape, pieces, low, largest):
    factor_of = 1.0
    for dim, shards_of in pieces:
        steps = jax.random.uniform(jax.random.fold_in(jax.random.fold_in(own_key, 6), dim), (shards_of,), jnp.float32, low / len(pieces), largest / len(pieces))
        factor_of = factor_of * jnp.repeat(jnp.exp(steps), shape[dim] // shards_of).reshape((-1,) + (1,) * (len(shape) - 1 - dim))
    return factor_of


def shared_out(stream_key, own, number, rows, number_of, top, limit, skew):
    sequence = jax.random.permutation(stream_key, number_of)
    heavy_load, common = load_shares(number_of, rows * top, limit, skew, True), load_shares(number_of, rows * top, limit, skew, False)
    places = jnp.arange(number_of)

    def named(tallies, rotation):
        used = int((tallies > 0).sum())
        fixed = max(1, used // 4)
        shifted = fixed + (places - fixed + rotation * (used - fixed)) % max(1, number_of - fixed)
        return jnp.zeros((number_of,), jnp.int32).at[sequence[jnp.where(places < fixed, places, shifted)]].set(jnp.asarray(tallies, jnp.int32))

    tallies = jnp.where(number % 4 == 0, named(heavy_load, number // 4), named(common, number - number // 4 - 1))
    mixed = jax.random.permutation(jax.random.fold_in(own, 3), number_of)
    donor, receiver = mixed[0:number_of // 2 * 2:2], mixed[1:number_of // 2 * 2:2]
    room = jnp.minimum(tallies[donor] - 1, limit - tallies[receiver]) // 2
    room = jnp.where((donor == sequence[0]) | (receiver == sequence[0]) | (tallies[receiver] == 0), 0, jnp.maximum(room, 0))
    shifted = jax.random.randint(jax.random.fold_in(own, 4), (number_of // 2,), 0, 1 << 20) % (room + 1)
    tallies = tallies.at[donor].add(-shifted).at[receiver].add(shifted)
    labels = jnp.searchsorted(jnp.cumsum(tallies), jnp.arange(rows * top), side="right").astype(jnp.int32)
    listing = labels.reshape(top, rows).T
    listing = listing[jax.random.permutation(jax.random.fold_in(own, 1), rows)]
    rotation = jax.random.randint(jax.random.fold_in(own, 2), (rows, 1), 0, top)
    return jnp.take_along_axis(listing, (jnp.arange(top)[None, :] + rotation) % top, axis=1)


def load_shares(count, total, most, lean, full):
    loads = [(1 << 20) // math.isqrt(grade ** lean) + 1 for grade in range(1, count + 1)]
    largest = most if full else min(most, max(-(-total // count), total * loads[0] // sum(loads)))
    least = 1 if total - largest >= count - 1 else 0
    counts, spare = [largest] + [least] * (count - 1), total - largest - least * (count - 1)
    while spare > 0:
        movable = [i for i in range(1, count) if counts[i] < largest] or [i for i in range(1, count) if counts[i] < most]
        mass, budget = sum([loads[i] for i in movable]), spare
        for i in movable:
            more = min(most - counts[i], max(1, budget * loads[i] // mass), spare)
            counts[i] = counts[i] + more
            spare = spare - more
    return np.array(counts)


def noise(own_key, shape, deviation, limit, split=(), held_as=jnp.bfloat16):
    values = deviation * jax.random.normal(own_key, shape, jnp.float32)
    if split:
        values = values * shard_levels(own_key, shape, split, -0.22, 0.18)
    return jnp.clip(values, -limit, limit).astype(held_as)


def setup_inputs(seed: int = 0, part: int = 0) -> dict:
    seeds = jax.random.split(jax.random.key(seed), 12)
    part_splits = jax.random.split(jax.random.fold_in(seeds[11], part), 12)
    current = noise(part_splits[0], (TOKENS, D), 1.0, 6.0, ((0, 8), (1, 2)))
    previous = noise(part_splits[1], (TOKENS, D), 1.0, 6.0, ((0, 8), (1, 2)), jnp.float32)
    expert_ids_keys = jax.random.split(jax.random.fold_in(part_splits[2], 1), TOKENS // TOK_DEV)
    expert_ids_turns = jax.random.permutation(jax.random.fold_in(part_splits[2], 3), TOKENS // TOK_DEV)
    expert_ids = jax.vmap(lambda own, number: shared_out(jax.random.fold_in(part_splits[2], 2), own, number, TOK_DEV, EXPERTS, TOP_K, CAP, 2))(expert_ids_keys, expert_ids_turns).reshape((TOKENS, TOP_K))
    gate_values = jnp.clip(0.1 + 0.9 * jax.random.uniform(part_splits[3], (TOKENS, TOP_K), jnp.float32) ** shard_levels(part_splits[3], (TOKENS, TOP_K), ((0, 8),), -0.2, 0.2), 0.1, 1.0)
    norm_gain = jnp.clip(1.0 + 0.18 * jax.random.normal(seeds[4], (D,), jnp.float32), 0.1, 1.9)
    expert_gate = noise(seeds[5], (EXPERTS, D, F), D ** -0.5, 0.125, ((0, 8), (1, 2)))
    expert_up = noise(seeds[6], (EXPERTS, D, F), D ** -0.5, 0.125, ((0, 8), (1, 2)))
    expert_down = noise(seeds[7], (EXPERTS, F, D), F ** -0.5, 0.21875, ((0, 8), (2, 2)))
    dense_gate = noise(seeds[8], (D, FFD), D ** -0.5, 0.125, ((0, 8), (1, 2)))
    dense_up = noise(seeds[9], (D, FFD), D ** -0.5, 0.125, ((0, 8), (1, 2)))
    dense_down = noise(seeds[10], (FFD, D), FFD ** -0.5, 0.109375, ((0, 2), (1, 8)))
    return {"current": current, "previous": previous, "expert_ids": expert_ids, "gate_values": gate_values, "norm_gain": norm_gain, "expert_gate": expert_gate, "expert_up": expert_up, "expert_down": expert_down, "dense_gate": dense_gate, "dense_up": dense_up, "dense_down": dense_down}


def block_positions(block_ids):
    flat_ids = block_ids.reshape(-1)
    one_hot = (flat_ids[:, None] == jnp.arange(EXPERTS, dtype=jnp.int32)[None, :]).astype(jnp.int32)
    before = jnp.cumsum(one_hot, axis=0) - one_hot
    return lax.optimization_barrier(jnp.sum(before * one_hot, axis=1)).astype(jnp.int32)

def reference(current, previous, expert_ids, gate_values, norm_gain, expert_gate, expert_up, expert_down, dense_gate, dense_up, dense_down):
    slice_width = D // N_HIDDEN
    per_expert = N_EXPERT * CAP
    routed = previous.astype(jnp.bfloat16)
    routed_pad = jnp.concatenate([routed, jnp.zeros((1, D), jnp.bfloat16)], axis=0)
    position = jax.vmap(block_positions)(expert_ids.reshape(N_EXPERT, TOK_DEV, TOP_K)).reshape(-1)
    flat_ids = expert_ids.reshape(-1).astype(jnp.int32)
    token_of = (jnp.arange(TOKENS * TOP_K, dtype=jnp.int32) // TOP_K).astype(jnp.int32)
    source = (token_of // TOK_DEV).astype(jnp.int32)
    place = (flat_ids * per_expert + source * CAP + position).astype(jnp.int32)
    table = jnp.full((EXPERTS * per_expert,), TOKENS, jnp.int32).at[place].set(token_of)
    table = table.reshape(EXPERTS, per_expert)

    def one_expert(inputs):
        rows_index, w_gate, w_up, w_down = inputs
        rows = routed_pad[rows_index].astype(jnp.float32).reshape(per_expert, N_HIDDEN, slice_width)
        gate_part = jnp.einsum('rhd,hdf->hrf', rows, w_gate.astype(jnp.float32).reshape(N_HIDDEN, slice_width, F))
        up_part = jnp.einsum('rhd,hdf->hrf', rows, w_up.astype(jnp.float32).reshape(N_HIDDEN, slice_width, F))
        gate_low = lax.optimization_barrier(gate_part.astype(jnp.bfloat16))
        up_low = lax.optimization_barrier(up_part.astype(jnp.bfloat16))
        gate_sum = lax.optimization_barrier(jnp.sum(gate_low.astype(jnp.float32), axis=0))
        up_sum = lax.optimization_barrier(jnp.sum(up_low.astype(jnp.float32), axis=0))
        act = (jax.nn.silu(gate_sum) * up_sum).astype(jnp.bfloat16)
        return jnp.dot(act, w_down, preferred_element_type=jnp.float32).astype(jnp.bfloat16)
    outputs = lax.map(one_expert, (table, expert_gate, expert_up, expert_down)).reshape(EXPERTS * per_expert, D)
    place_grid = place.reshape(TOKENS, TOP_K)
    routed_sum = jnp.zeros((TOKENS, D), jnp.float32)
    for choice_index in range(TOP_K):
        picked = outputs[place_grid[:, choice_index]].astype(jnp.float32)
        routed_sum = routed_sum + gate_values[:, choice_index][:, None] * picked
    wide = current.astype(jnp.float32)
    mean_square = lax.optimization_barrier(jnp.mean(wide * wide, axis=1, keepdims=True))
    normed = (wide * norm_gain[None, :] / jnp.sqrt(mean_square + 1e-06)).astype(jnp.bfloat16)
    gate_dense = jnp.dot(normed, dense_gate, preferred_element_type=jnp.float32)
    up_dense = jnp.dot(normed, dense_up, preferred_element_type=jnp.float32)
    dense_act = (jax.nn.silu(gate_dense) * up_dense).astype(jnp.bfloat16)
    share = FFD // N_HIDDEN
    dense_sum = jnp.zeros((TOKENS, D), jnp.float32)
    for part_index in range(N_HIDDEN):
        term = jnp.dot(dense_act[:, part_index * share:(part_index + 1) * share], dense_down[part_index * share:(part_index + 1) * share], preferred_element_type=jnp.float32)
        term_low = lax.optimization_barrier(term.astype(jnp.bfloat16))
        dense_sum = dense_sum + term_low.astype(jnp.float32)
    return (dense_sum + routed_sum).astype(jnp.bfloat16)
```

```python
import jax
import jax.numpy as jnp
from jax import lax
from jax.sharding import PartitionSpec as P


def own_gates(expert_ids, gate_values, experts_all):
    hit = expert_ids[:, :, None] == jnp.arange(experts_all, dtype=jnp.int32)[None, None, :]
    return jnp.sum(jnp.where(hit, gate_values[:, :, None], 0.0), axis=1)


def normalize(current, norm_gain):
    width = current.shape[1]
    wide = current.astype(jnp.float32)
    total = lax.psum(jnp.sum(wide * wide, axis=1, keepdims=True), "hidden")
    mean_square = total / norm_gain.shape[0]
    gain = lax.dynamic_slice_in_dim(norm_gain, lax.axis_index("hidden") * width, width)
    return (wide * gain[None, :] / jnp.sqrt(mean_square + 1e-06)).astype(jnp.bfloat16)


def swiglu(rows, gate, up):
    gate_sum = jnp.dot(rows, gate, preferred_element_type=jnp.float32)
    up_sum = jnp.dot(rows, up, preferred_element_type=jnp.float32)
    return jax.nn.silu(gate_sum) * up_sum


def local(
    current,
    previous,
    expert_ids,
    gate_values,
    norm_gain,
    expert_gate,
    expert_up,
    expert_down,
    dense_gate,
    dense_up,
    dense_down,
):
    owned = expert_gate.shape[0]
    owners = lax.axis_size("expert")
    bf16 = jnp.bfloat16
    routed = previous.astype(bf16)
    normed = normalize(current, norm_gain)
    gates = own_gates(expert_ids, gate_values, owned * owners)
    swap = lambda w, axis, cut, join: lax.all_to_all(w, axis, split_axis=cut, concat_axis=join, tiled=True)
    wg = swap(expert_gate, "hidden", 2, 1)
    wu = swap(expert_up, "hidden", 2, 1)
    wd = swap(expert_down, "hidden", 1, 2)
    both = lax.all_gather(jnp.stack([routed, normed]), "expert", axis=1, tiled=True)
    both = lax.all_gather(both, "hidden", axis=2, tiled=True)
    mine = swap(gates, "expert", 1, 0)
    dg = swap(dense_gate, "expert", 1, 0)
    du = swap(dense_up, "expert", 1, 0)
    dd = swap(dense_down, "expert", 0, 1)
    acts = [
        (swiglu(both[0], wg[j], wu[j]) * mine[:, j : j + 1]).astype(bf16) for j in range(owned)
    ]
    acts.append(swiglu(both[1], dg, du).astype(bf16))
    downs = [wd[j] for j in range(owned)] + [dd]
    total = jnp.dot(
        jnp.concatenate(acts, axis=1), jnp.concatenate(downs, axis=0), preferred_element_type=jnp.float32
    ).astype(bf16)
    half = lax.psum_scatter(total, "hidden", scatter_dimension=1, tiled=True)
    return lax.psum_scatter(half, "expert", scatter_dimension=0, tiled=True)


def solution(mesh):
    placed = (
        P(("groups", "expert"), "hidden"),
        P(("groups", "expert"), "hidden"),
        P(("groups", "expert"), None),
        P(("groups", "expert"), None),
        P(),
        P("expert", "hidden", None),
        P("expert", "hidden", None),
        P("expert", None, "hidden"),
        P("expert", "hidden"),
        P("expert", "hidden"),
        P("hidden", "expert"),
    )
    return jax.shard_map(
        local,
        mesh=mesh,
        in_specs=placed,
        out_specs=P(("groups", "expert"), "hidden"),
        check_vma=False,
    )
```

```python
import functools

import jax
import jax.numpy as jnp
from jax import lax
from jax.experimental import pallas as pl
from jax.experimental.pallas import tpu as pltpu
from jax.sharding import PartitionSpec as P

MESH = pl.DeviceIdType.MESH


def ring_place(index, n):
    odd = lax.rem(index, 2)
    level = lax.div(index, 2)
    return (1 - odd) * level + odd * (n - 1 - level)


def ring_index(place, n):
    place = lax.rem(place + 2 * n, n)
    back = lax.div(place, n // 2)
    return (1 - back) * 2 * place + back * (2 * (n - 1 - place) + 1)


def rows_of(index, size):
    return pl.ds(pl.multiple_of(index * size, size), size)


def greet(peers):
    barrier = pltpu.get_barrier_semaphore()
    for peer in peers:
        pl.semaphore_signal(barrier, inc=1, device_id=peer, device_id_type=MESH)
    pl.semaphore_wait(barrier, len(peers))


def remote(src, dst, send, recv, peer):
    return pltpu.make_async_remote_copy(
        src_ref=src, dst_ref=dst, send_sem=send, recv_sem=recv, device_id=peer, device_id_type=MESH
    )


def gather_kernel(
    n, tok, gates, gu, dn, eg, eu, ed, all_tok, all_gates, w1, wd, w2,
    ring_s, ring_r, core_s, core_r, exp_s, exp_r, push_s, push_r, fwd_s, fwd_r, here,
):
    me, h, g = lax.axis_index("expert"), lax.axis_index("hidden"), lax.axis_index("groups")
    kinds, tokens, width = tok.shape
    owned, _, hidden_units = eg.shape
    share = hidden_units // 2
    depth, units = gu.shape[1], dn.shape[1]
    half = n // 2
    place = ring_place(me, n)
    right, left = {"expert": ring_index(place + 1, n)}, {"expert": ring_index(place - 1, n)}
    mate, twin = {"hidden": 1 - h}, {"groups": 1 - g}
    greet([{"expert": lax.rem(me + d, n)} for d in range(1, n)] + [mate, twin])
    pending = []
    mine = pl.ds(pl.multiple_of(h * width, width), width)

    def start(copy):
        copy.start()
        pending.append(copy)

    def block(t, origin, lo, size):
        rows = pl.ds(pl.multiple_of(origin * tokens + lo, size), size)
        return all_tok.at[t, rows, mine]

    def span(step, way):
        if step < half:
            return 0, tokens
        return way * (tokens // 2), tokens // 2

    def hop(t, step, way):
        origin = ring_index(place - (step - 1) if way == 0 else place + (step - 1), n)
        lo, size = span(step, way)
        src = tok.at[t, pl.ds(lo, size)] if step == 1 else block(t, origin, lo, size)
        k = (t * 2 + way) * half + step - 1
        return remote(src, block(t, origin, lo, size), ring_s.at[k], ring_r.at[k], right if way == 0 else left)

    def to_mate(t, origin, lo, size, k, src=None):
        view = block(t, origin, lo, size)
        k = t * (n + 1) + k
        start(remote(view if src is None else src, view, core_s.at[k], core_r.at[k], mate))

    for t in range(kinds):
        for way in range(2):
            start(hop(t, 1, way))
    locals_ = []

    def keep(src, dst):
        copy = pltpu.make_async_copy(src, dst, here.at[len(locals_)])
        copy.start()
        locals_.append(copy)

    pushes = []
    for d in range(1, n):
        to = lax.rem(me + d, n)
        peer = {"expert": to}
        rows = pl.ds(pl.multiple_of(g * (depth // 2), depth // 2), depth // 2)
        into = pl.ds(pl.multiple_of(me * depth + g * (depth // 2), depth // 2), depth // 2)
        a = remote(gu.at[to, rows], wd.at[into], push_s.at[3 * d], push_r.at[3 * d], peer)
        rows = pl.ds(pl.multiple_of(g * (units // 2), units // 2), units // 2)
        into = pl.ds(pl.multiple_of(owned * share + g * (units // 2), 16), units // 2)
        b = remote(
            dn.at[to, rows], w2.at[into, rows_of(me, depth)], push_s.at[3 * d + 1], push_r.at[3 * d + 1], peer
        )
        c = remote(gates.at[to], all_gates.at[me], push_s.at[3 * d + 2], push_r.at[3 * d + 2], peer)
        for copy in (a, b, c):
            copy.start()
        pushes.append((a, b, c))
    swaps = []
    for j in range(owned):
        away = pl.ds(pl.multiple_of((1 - h) * share, 128), share)
        stay = pl.ds(pl.multiple_of(h * share, 128), share)
        for i, w in enumerate((eg, eu)):
            spot = w1.at[rows_of(h, width), pl.ds((2 * j + i) * share, share)]
            k = 3 * j + i
            swaps.append(remote(w.at[j, :, away], spot, exp_s.at[k], exp_r.at[k], mate))
            keep(w.at[j, :, stay], spot)
        spot = w2.at[pl.ds(j * share, share), mine]
        away = pl.ds(pl.multiple_of((1 - h) * share, 16), share)
        stay = pl.ds(pl.multiple_of(h * share, 16), share)
        swaps.append(remote(ed.at[j, away], spot, exp_s.at[3 * j + 2], exp_r.at[3 * j + 2], mate))
        keep(ed.at[j, stay], spot)
    for copy in swaps:
        copy.start()
    for t in range(kinds):
        to_mate(t, me, 0, tokens, 0, tok.at[t])
        keep(tok.at[t], block(t, me, 0, tokens))
    keep(gu.at[me], wd.at[rows_of(me, depth)])
    keep(dn.at[me], w2.at[pl.ds(owned * share, units), rows_of(me, depth)])
    keep(gates.at[me], all_gates.at[me])

    forwards = []

    def pass_on(d):
        for copy in pushes[d - 1]:
            copy.wait_recv()
        source = lax.rem(me - d + n, n)
        into = pl.ds(pl.multiple_of(source * depth + g * (depth // 2), depth // 2), depth // 2)
        a = remote(wd.at[into], wd.at[into], fwd_s.at[2 * d], fwd_r.at[2 * d], twin)
        into = pl.ds(pl.multiple_of(owned * share + g * (units // 2), 16), units // 2)
        spot = w2.at[into, rows_of(source, depth)]
        b = remote(spot, spot, fwd_s.at[2 * d + 1], fwd_r.at[2 * d + 1], twin)
        for copy in (a, b):
            copy.start()
            forwards.append(copy)

    late = list(range(1, n))
    for step in range(1, half + 1):
        for t in range(kinds):
            for way in range(2):
                hop(t, step, way).wait_recv()
                origin = ring_index(place - step if way == 0 else place + step, n)
                lo, size = span(step, way)
                if step < half:
                    start(hop(t, step + 1, way))
                to_mate(t, origin, lo, size, 2 * step - 1 + way)
        if step > 1 and step < half:
            for _ in range(2):
                pass_on(late.pop(0))
    while late:
        pass_on(late.pop(0))
    for copy in pending:
        copy.wait_send()
    for t in range(kinds):
        for k in range(n + 1):
            step, way = (k + 1) // 2, (k + 1) % 2
            lo, size = (0, tokens) if k == 0 else span(step, way)
            origin = ring_index(place if k == 0 else (place - step if way == 0 else place + step), n)
            theirs = pl.ds(pl.multiple_of((1 - h) * width, width), width)
            rows = pl.ds(pl.multiple_of(origin * tokens + lo, size), size)
            view = all_tok.at[t, rows, theirs]
            remote(view, view, core_s.at[t * (n + 1) + k], core_r.at[t * (n + 1) + k], mate).wait_recv()
    for copy in swaps + forwards:
        copy.wait()
    for group in pushes:
        for copy in group:
            copy.wait_send()
    for copy in locals_:
        copy.wait()


def gather(n, tok, gates, gu, dn, eg, eu, ed):
    kinds, tokens, width = tok.shape
    owned, _, hidden_units = eg.shape
    depth, units = gu.shape[1], dn.shape[1]
    share = hidden_units // 2
    dma = lambda count: pltpu.SemaphoreType.DMA((count,))
    shape = jax.ShapeDtypeStruct
    bf16 = jnp.bfloat16
    return pl.pallas_call(
        functools.partial(gather_kernel, n),
        out_shape=(
            shape((kinds, n * tokens, 2 * width), bf16),
            shape(gates.shape, gates.dtype),
            shape((2 * width, 2 * owned * share), bf16),
            shape((n * depth, gu.shape[2]), bf16),
            shape((owned * share + units, 2 * width), bf16),
        ),
        in_specs=[pl.BlockSpec(memory_space=pl.ANY)] * 7,
        out_specs=[pl.BlockSpec(memory_space=pl.ANY)] * 5,
        scratch_shapes=[dma(kinds * n)] * 2
        + [dma(kinds * (n + 1))] * 2
        + [dma(3 * owned)] * 2
        + [dma(3 * n)] * 2
        + [dma(2 * n)] * 2
        + [dma(3 * owned + kinds + 3)],
        compiler_params=pltpu.CompilerParams(collective_id=0, has_side_effects=True),
    )(tok, gates, gu, dn, eg, eu, ed)


def reduce_kernel(n, part, out, core, sent, got, core_s, core_r, ring_s, ring_r):
    me, h = lax.axis_index("expert"), lax.axis_index("hidden")
    tokens, width = out.shape
    half = n // 2
    place = ring_place(me, n)
    right, left = {"expert": ring_index(place + 1, n)}, {"expert": ring_index(place - 1, n)}
    mate = {"hidden": 1 - h}
    greet([right, left, mate])
    mine = pl.ds(pl.multiple_of(h * width, width), width)
    theirs = pl.ds(pl.multiple_of((1 - h) * width, width), width)
    order = [half]
    for d in range(half - 1, 0, -1):
        order += [d, -d]
    order.append(0)
    trades = {}
    for k, d in enumerate(order):
        rows = rows_of(ring_index(place + d, n), tokens)
        trades[d] = remote(part.at[rows, theirs], core.at[rows], core_s.at[k], core_r.at[k], mate)
        trades[d].start()

    def own(d):
        trades[d].wait_recv()
        rows = rows_of(ring_index(place + d, n), tokens)
        return part[rows, mine].astype(jnp.float32) + core[rows].astype(jnp.float32)

    def view(buffer, step, way):
        k = way * half + step - 1
        if step == 1:
            return buffer.at[k, pl.ds(way * (tokens // 2), tokens // 2)]
        return buffer.at[k]

    def hop(step, way):
        k = way * half + step - 1
        return remote(
            view(sent, step, way), view(got, step, way), ring_s.at[k], ring_r.at[k], right if way == 0 else left
        )

    far = own(half).astype(jnp.bfloat16)
    hops = []
    for step in range(1, half + 1):
        for way in range(2):
            k = way * half + step - 1
            if step == 1:
                lo = way * (tokens // 2)
                sent[k, pl.ds(lo, tokens // 2)] = far[lo : lo + tokens // 2]
            else:
                d = half + 1 - step
                value = own(d if way == 0 else -d)
                hop(step - 1, way).wait_recv()
                if step == 2:
                    lo = way * (tokens // 2)
                    other = tokens // 2 - lo
                    cut = slice(lo, lo + tokens // 2)
                    add = got[k - 1, pl.ds(lo, tokens // 2)].astype(jnp.float32)
                    sent[k, pl.ds(lo, tokens // 2)] = (value[cut] + add).astype(jnp.bfloat16)
                    sent[k, pl.ds(other, tokens // 2)] = value[other : other + tokens // 2].astype(jnp.bfloat16)
                else:
                    sent[k] = (value + got[k - 1].astype(jnp.float32)).astype(jnp.bfloat16)
            copy = hop(step, way)
            copy.start()
            hops.append(copy)
    value = own(0)
    for way in range(2):
        hop(half, way).wait_recv()
        value = value + got[way * half + half - 1].astype(jnp.float32)
    out[...] = value.astype(jnp.bfloat16)
    for copy in hops:
        copy.wait_send()
    for copy in trades.values():
        copy.wait_send()


def reduce_sum(n, part):
    tokens, width = part.shape[0] // n, part.shape[1] // 2
    bf16 = jnp.bfloat16
    dma = lambda count: pltpu.SemaphoreType.DMA((count,))
    return pl.pallas_call(
        functools.partial(reduce_kernel, n),
        out_shape=jax.ShapeDtypeStruct((tokens, width), bf16),
        in_specs=[pl.BlockSpec(memory_space=pltpu.VMEM)],
        out_specs=pl.BlockSpec(memory_space=pltpu.VMEM),
        scratch_shapes=[
            pltpu.VMEM((n * tokens, width), bf16),
            pltpu.VMEM((n, tokens, width), bf16),
            pltpu.VMEM((n, tokens, width), bf16),
            dma(n), dma(n), dma(n), dma(n),
        ],
        compiler_params=pltpu.CompilerParams(
            collective_id=1, has_side_effects=True, vmem_limit_bytes=40 * 2**20
        ),
    )(part)


def kernel_fits(tokens, width, share, depth, units):
    pairs = lax.axis_size("hidden") == 2 and lax.axis_size("groups") == 2
    even = lax.axis_size("expert") % 2 == 0 and lax.axis_size("expert") >= 4
    aligned = tokens % 128 == 0 and width % 128 == 0 and share % 128 == 0
    return pairs and even and aligned and depth % 128 == 0 and units % 32 == 0


def by_kernels(routed, normed, gates, expert_gate, expert_up, expert_down, dense_gate, dense_up, dense_down):
    n = lax.axis_size("expert")
    tokens = routed.shape[0]
    owned, _, hidden_units = expert_gate.shape
    share = hidden_units // 2
    depth, spread = dense_gate.shape
    units = spread // n
    bf16 = jnp.bfloat16
    cut = lambda w: w.reshape(depth, n, units).transpose(1, 0, 2)
    gu = jnp.concatenate([cut(dense_gate), cut(dense_up)], axis=2)
    dn = dense_down.reshape(n, units, depth)
    pad = -owned % 8
    packed = jnp.pad(gates.T.reshape(n, owned, tokens), ((0, 0), (0, pad), (0, 0)))
    rows, got, w1, wd, w2 = gather(
        n, jnp.stack([routed, normed]), packed, gu, dn, expert_gate, expert_up, expert_down
    )
    scale = got[:, :owned].transpose(0, 2, 1).reshape(n * tokens, owned)
    sums = jnp.dot(rows[0], w1, preferred_element_type=jnp.float32)
    dense = jnp.dot(rows[1], wd, preferred_element_type=jnp.float32)
    acts = []
    for j in range(owned):
        gate = sums[:, 2 * j * share : (2 * j + 1) * share]
        up = sums[:, (2 * j + 1) * share : (2 * j + 2) * share]
        acts.append((jax.nn.silu(gate) * up * scale[:, j : j + 1]).astype(bf16))
    acts.append((jax.nn.silu(dense[:, :units]) * dense[:, units:]).astype(bf16))
    part = jnp.dot(jnp.concatenate(acts, axis=1), w2, preferred_element_type=jnp.float32)
    return reduce_sum(n, part.astype(bf16))


def own_gates(expert_ids, gate_values, experts_all):
    hit = expert_ids[:, :, None] == jnp.arange(experts_all, dtype=jnp.int32)[None, None, :]
    return jnp.sum(jnp.where(hit, gate_values[:, :, None], 0.0), axis=1)


def normalize(current, norm_gain):
    width = current.shape[1]
    wide = current.astype(jnp.float32)
    total = lax.psum(jnp.sum(wide * wide, axis=1, keepdims=True), "hidden")
    mean_square = total / norm_gain.shape[0]
    gain = lax.dynamic_slice_in_dim(norm_gain, lax.axis_index("hidden") * width, width)
    return (wide * gain[None, :] / jnp.sqrt(mean_square + 1e-06)).astype(jnp.bfloat16)


def swiglu(rows, gate, up):
    gate_sum = jnp.dot(rows, gate, preferred_element_type=jnp.float32)
    up_sum = jnp.dot(rows, up, preferred_element_type=jnp.float32)
    return jax.nn.silu(gate_sum) * up_sum


def local(
    current,
    previous,
    expert_ids,
    gate_values,
    norm_gain,
    expert_gate,
    expert_up,
    expert_down,
    dense_gate,
    dense_up,
    dense_down,
):
    owned = expert_gate.shape[0]
    owners = lax.axis_size("expert")
    bf16 = jnp.bfloat16
    routed = previous.astype(bf16)
    normed = normalize(current, norm_gain)
    gates = own_gates(expert_ids, gate_values, owned * owners)
    share, units = expert_gate.shape[2] // 2, dense_gate.shape[1] // owners
    if kernel_fits(*routed.shape, share, dense_gate.shape[0], units):
        return by_kernels(
            routed, normed, gates, expert_gate, expert_up, expert_down, dense_gate, dense_up, dense_down
        )
    swap = lambda w, axis, cut, join: lax.all_to_all(w, axis, split_axis=cut, concat_axis=join, tiled=True)
    wg = swap(expert_gate, "hidden", 2, 1)
    wu = swap(expert_up, "hidden", 2, 1)
    wd = swap(expert_down, "hidden", 1, 2)
    both = lax.all_gather(jnp.stack([routed, normed]), "expert", axis=1, tiled=True)
    both = lax.all_gather(both, "hidden", axis=2, tiled=True)
    mine = swap(gates, "expert", 1, 0)
    dg = swap(dense_gate, "expert", 1, 0)
    du = swap(dense_up, "expert", 1, 0)
    dd = swap(dense_down, "expert", 0, 1)
    acts = [
        (swiglu(both[0], wg[j], wu[j]) * mine[:, j : j + 1]).astype(bf16) for j in range(owned)
    ]
    acts.append(swiglu(both[1], dg, du).astype(bf16))
    downs = [wd[j] for j in range(owned)] + [dd]
    total = jnp.dot(
        jnp.concatenate(acts, axis=1), jnp.concatenate(downs, axis=0), preferred_element_type=jnp.float32
    ).astype(bf16)
    half = lax.psum_scatter(total, "hidden", scatter_dimension=1, tiled=True)
    return lax.psum_scatter(half, "expert", scatter_dimension=0, tiled=True)


def solution(mesh):
    placed = (
        P(("groups", "expert"), "hidden"),
        P(("groups", "expert"), "hidden"),
        P(("groups", "expert"), None),
        P(("groups", "expert"), None),
        P(),
        P("expert", "hidden", None),
        P("expert", "hidden", None),
        P("expert", None, "hidden"),
        P("expert", "hidden"),
        P("expert", "hidden"),
        P("hidden", "expert"),
    )
    return jax.shard_map(
        local,
        mesh=mesh,
        in_specs=placed,
        out_specs=P(("groups", "expert"), "hidden"),
        check_vma=False,
    )
```

```python
import functools

import jax
import jax.numpy as jnp
from jax import lax
from jax.experimental import pallas as pl
from jax.experimental.pallas import tpu as pltpu
from jax.sharding import PartitionSpec as P

MESH = pl.DeviceIdType.MESH


def ring_place(index, n):
    odd = lax.rem(index, 2)
    level = lax.div(index, 2)
    return (1 - odd) * level + odd * (n - 1 - level)


def ring_index(place, n):
    place = lax.rem(place + 2 * n, n)
    back = lax.div(place, n // 2)
    return (1 - back) * 2 * place + back * (2 * (n - 1 - place) + 1)


def rows_of(index, size):
    return pl.ds(pl.multiple_of(index * size, size), size)


def greet(peers):
    barrier = pltpu.get_barrier_semaphore()
    for peer in peers:
        pl.semaphore_signal(barrier, inc=1, device_id=peer, device_id_type=MESH)
    pl.semaphore_wait(barrier, len(peers))


def remote(src, dst, send, recv, peer):
    return pltpu.make_async_remote_copy(
        src_ref=src, dst_ref=dst, send_sem=send, recv_sem=recv, device_id=peer, device_id_type=MESH
    )


def gather_kernel(
    n, tok, gates, gu, dn, eg, eu, ed, all_tok, all_gates, w1, wd, w2,
    ring_s, ring_r, core_s, core_r, exp_s, exp_r, push_s, push_r, fwd_s, fwd_r, here,
):
    me, h, g = lax.axis_index("expert"), lax.axis_index("hidden"), lax.axis_index("groups")
    kinds, tokens, width = tok.shape
    owned, _, hidden_units = eg.shape
    share = hidden_units // 2
    depth, units = gu.shape[1], dn.shape[1]
    half = n // 2
    place = ring_place(me, n)
    right, left = {"expert": ring_index(place + 1, n)}, {"expert": ring_index(place - 1, n)}
    mate, twin = {"hidden": 1 - h}, {"groups": 1 - g}
    greet([{"expert": lax.rem(me + d, n)} for d in range(1, n)] + [mate, twin])
    pending = []
    mine = pl.ds(pl.multiple_of(h * width, width), width)

    def start(copy):
        copy.start()
        pending.append(copy)

    def block(t, origin, lo, size):
        rows = pl.ds(pl.multiple_of(origin * tokens + lo, size), size)
        return all_tok.at[t, rows, mine]

    def span(step, way):
        if step < half:
            return 0, tokens
        return way * (tokens // 2), tokens // 2

    def hop(t, step, way):
        origin = ring_index(place - (step - 1) if way == 0 else place + (step - 1), n)
        lo, size = span(step, way)
        src = tok.at[t, pl.ds(lo, size)] if step == 1 else block(t, origin, lo, size)
        k = (t * 2 + way) * half + step - 1
        return remote(src, block(t, origin, lo, size), ring_s.at[k], ring_r.at[k], right if way == 0 else left)

    def to_mate(t, origin, lo, size, k, src=None):
        view = block(t, origin, lo, size)
        k = t * (n + 1) + k
        start(remote(view if src is None else src, view, core_s.at[k], core_r.at[k], mate))

    for t in range(kinds):
        for way in range(2):
            start(hop(t, 1, way))
    locals_ = []

    def keep(src, dst):
        copy = pltpu.make_async_copy(src, dst, here.at[len(locals_)])
        copy.start()
        locals_.append(copy)

    pushes = []
    for d in range(1, n):
        to = lax.rem(me + d, n)
        peer = {"expert": to}
        rows = pl.ds(pl.multiple_of(g * (depth // 2), depth // 2), depth // 2)
        into = pl.ds(pl.multiple_of(me * depth + g * (depth // 2), depth // 2), depth // 2)
        a = remote(gu.at[to, rows], wd.at[into], push_s.at[3 * d], push_r.at[3 * d], peer)
        rows = pl.ds(pl.multiple_of(g * (units // 2), units // 2), units // 2)
        into = pl.ds(pl.multiple_of(owned * share + g * (units // 2), 16), units // 2)
        b = remote(
            dn.at[to, rows], w2.at[into, rows_of(me, depth)], push_s.at[3 * d + 1], push_r.at[3 * d + 1], peer
        )
        c = remote(gates.at[to], all_gates.at[me], push_s.at[3 * d + 2], push_r.at[3 * d + 2], peer)
        for copy in (a, b, c):
            copy.start()
        pushes.append((a, b, c))
    swaps = []

    def swap_expert(j):
        away = pl.ds(pl.multiple_of((1 - h) * share, 128), share)
        stay = pl.ds(pl.multiple_of(h * share, 128), share)
        for i, w in enumerate((eg, eu)):
            spot = w1.at[rows_of(h, width), pl.ds((2 * j + i) * share, share)]
            k = 3 * j + i
            swaps.append(remote(w.at[j, :, away], spot, exp_s.at[k], exp_r.at[k], mate))
            swaps[-1].start()
            keep(w.at[j, :, stay], spot)
        spot = w2.at[pl.ds(j * share, share), mine]
        away = pl.ds(pl.multiple_of((1 - h) * share, 16), share)
        stay = pl.ds(pl.multiple_of(h * share, 16), share)
        swaps.append(remote(ed.at[j, away], spot, exp_s.at[3 * j + 2], exp_r.at[3 * j + 2], mate))
        swaps[-1].start()
        keep(ed.at[j, stay], spot)

    for t in range(kinds):
        to_mate(t, me, 0, tokens, 0, tok.at[t])
        keep(tok.at[t], block(t, me, 0, tokens))
    keep(gu.at[me], wd.at[rows_of(me, depth)])
    keep(dn.at[me], w2.at[pl.ds(owned * share, units), rows_of(me, depth)])
    keep(gates.at[me], all_gates.at[me])

    forwards = []

    def pass_on(d):
        for copy in pushes[d - 1]:
            copy.wait_recv()
        source = lax.rem(me - d + n, n)
        into = pl.ds(pl.multiple_of(source * depth + g * (depth // 2), depth // 2), depth // 2)
        a = remote(wd.at[into], wd.at[into], fwd_s.at[2 * d], fwd_r.at[2 * d], twin)
        into = pl.ds(pl.multiple_of(owned * share + g * (units // 2), 16), units // 2)
        spot = w2.at[into, rows_of(source, depth)]
        b = remote(spot, spot, fwd_s.at[2 * d + 1], fwd_r.at[2 * d + 1], twin)
        for copy in (a, b):
            copy.start()
            forwards.append(copy)

    late = list(range(1, n))
    for step in range(1, half + 1):
        for t in range(kinds):
            for way in range(2):
                hop(t, step, way).wait_recv()
                origin = ring_index(place - step if way == 0 else place + step, n)
                lo, size = span(step, way)
                if step < half:
                    start(hop(t, step + 1, way))
                to_mate(t, origin, lo, size, 2 * step - 1 + way)
        for j in range(owned):
            if min(j + 1, half - 1) == step:
                swap_expert(j)
        if step == half - 1:
            for _ in range(half - 1):
                pass_on(late.pop(0))
    while late:
        pass_on(late.pop(0))
    for copy in pending:
        copy.wait_send()
    for t in range(kinds):
        for k in range(n + 1):
            step, way = (k + 1) // 2, (k + 1) % 2
            lo, size = (0, tokens) if k == 0 else span(step, way)
            origin = ring_index(place if k == 0 else (place - step if way == 0 else place + step), n)
            theirs = pl.ds(pl.multiple_of((1 - h) * width, width), width)
            rows = pl.ds(pl.multiple_of(origin * tokens + lo, size), size)
            view = all_tok.at[t, rows, theirs]
            remote(view, view, core_s.at[t * (n + 1) + k], core_r.at[t * (n + 1) + k], mate).wait_recv()
    for copy in swaps + forwards:
        copy.wait()
    for group in pushes:
        for copy in group:
            copy.wait_send()
    for copy in locals_:
        copy.wait()


def gather(n, tok, gates, gu, dn, eg, eu, ed):
    kinds, tokens, width = tok.shape
    owned, _, hidden_units = eg.shape
    depth, units = gu.shape[1], dn.shape[1]
    share = hidden_units // 2
    dma = lambda count: pltpu.SemaphoreType.DMA((count,))
    shape = jax.ShapeDtypeStruct
    bf16 = jnp.bfloat16
    return pl.pallas_call(
        functools.partial(gather_kernel, n),
        out_shape=(
            shape((kinds, n * tokens, 2 * width), bf16),
            shape(gates.shape, gates.dtype),
            shape((2 * width, 2 * owned * share), bf16),
            shape((n * depth, gu.shape[2]), bf16),
            shape((owned * share + units, 2 * width), bf16),
        ),
        in_specs=[pl.BlockSpec(memory_space=pl.ANY)] * 7,
        out_specs=[pl.BlockSpec(memory_space=pl.ANY)] * 5,
        scratch_shapes=[dma(kinds * n)] * 2
        + [dma(kinds * (n + 1))] * 2
        + [dma(3 * owned)] * 2
        + [dma(3 * n)] * 2
        + [dma(2 * n)] * 2
        + [dma(3 * owned + kinds + 3)],
        compiler_params=pltpu.CompilerParams(collective_id=0, has_side_effects=True),
    )(tok, gates, gu, dn, eg, eu, ed)


def reduce_kernel(n, part, out, core, sent, got, core_s, core_r, ring_s, ring_r):
    me, h = lax.axis_index("expert"), lax.axis_index("hidden")
    tokens, width = out.shape
    half = n // 2
    place = ring_place(me, n)
    right, left = {"expert": ring_index(place + 1, n)}, {"expert": ring_index(place - 1, n)}
    mate = {"hidden": 1 - h}
    greet([right, left, mate])
    mine = pl.ds(pl.multiple_of(h * width, width), width)
    theirs = pl.ds(pl.multiple_of((1 - h) * width, width), width)
    order = [half]
    for d in range(half - 1, 0, -1):
        order += [d, -d]
    order.append(0)
    trades = {}
    for k, d in enumerate(order):
        rows = rows_of(ring_index(place + d, n), tokens)
        trades[d] = remote(part.at[rows, theirs], core.at[rows], core_s.at[k], core_r.at[k], mate)
        trades[d].start()

    def own(d):
        trades[d].wait_recv()
        rows = rows_of(ring_index(place + d, n), tokens)
        return part[rows, mine].astype(jnp.float32) + core[rows].astype(jnp.float32)

    def view(buffer, step, way):
        k = way * half + step - 1
        if step == 1:
            return buffer.at[k, pl.ds(way * (tokens // 2), tokens // 2)]
        return buffer.at[k]

    def hop(step, way):
        k = way * half + step - 1
        return remote(
            view(sent, step, way), view(got, step, way), ring_s.at[k], ring_r.at[k], right if way == 0 else left
        )

    far = own(half).astype(jnp.bfloat16)
    hops = []
    for step in range(1, half + 1):
        for way in range(2):
            k = way * half + step - 1
            if step == 1:
                lo = way * (tokens // 2)
                sent[k, pl.ds(lo, tokens // 2)] = far[lo : lo + tokens // 2]
            else:
                d = half + 1 - step
                value = own(d if way == 0 else -d)
                hop(step - 1, way).wait_recv()
                if step == 2:
                    lo = way * (tokens // 2)
                    other = tokens // 2 - lo
                    cut = slice(lo, lo + tokens // 2)
                    add = got[k - 1, pl.ds(lo, tokens // 2)].astype(jnp.float32)
                    sent[k, pl.ds(lo, tokens // 2)] = (value[cut] + add).astype(jnp.bfloat16)
                    sent[k, pl.ds(other, tokens // 2)] = value[other : other + tokens // 2].astype(jnp.bfloat16)
                else:
                    sent[k] = (value + got[k - 1].astype(jnp.float32)).astype(jnp.bfloat16)
            copy = hop(step, way)
            copy.start()
            hops.append(copy)
    value = own(0)
    for way in range(2):
        hop(half, way).wait_recv()
        value = value + got[way * half + half - 1].astype(jnp.float32)
    out[...] = value.astype(jnp.bfloat16)
    for copy in hops:
        copy.wait_send()
    for copy in trades.values():
        copy.wait_send()


def reduce_sum(n, part):
    tokens, width = part.shape[0] // n, part.shape[1] // 2
    bf16 = jnp.bfloat16
    dma = lambda count: pltpu.SemaphoreType.DMA((count,))
    return pl.pallas_call(
        functools.partial(reduce_kernel, n),
        out_shape=jax.ShapeDtypeStruct((tokens, width), bf16),
        in_specs=[pl.BlockSpec(memory_space=pltpu.VMEM)],
        out_specs=pl.BlockSpec(memory_space=pltpu.VMEM),
        scratch_shapes=[
            pltpu.VMEM((n * tokens, width), bf16),
            pltpu.VMEM((n, tokens, width), bf16),
            pltpu.VMEM((n, tokens, width), bf16),
            dma(n), dma(n), dma(n), dma(n),
        ],
        compiler_params=pltpu.CompilerParams(
            collective_id=1, has_side_effects=True, vmem_limit_bytes=40 * 2**20
        ),
    )(part)


def kernel_fits(tokens, width, share, depth, units):
    pairs = lax.axis_size("hidden") == 2 and lax.axis_size("groups") == 2
    even = lax.axis_size("expert") % 2 == 0 and lax.axis_size("expert") >= 4
    aligned = tokens % 128 == 0 and width % 128 == 0 and share % 128 == 0
    return pairs and even and aligned and depth % 128 == 0 and units % 32 == 0


def by_kernels(routed, normed, gates, expert_gate, expert_up, expert_down, dense_gate, dense_up, dense_down):
    n = lax.axis_size("expert")
    tokens = routed.shape[0]
    owned, _, hidden_units = expert_gate.shape
    share = hidden_units // 2
    depth, spread = dense_gate.shape
    units = spread // n
    bf16 = jnp.bfloat16
    cut = lambda w: w.reshape(depth, n, units).transpose(1, 0, 2)
    gu = jnp.concatenate([cut(dense_gate), cut(dense_up)], axis=2)
    dn = dense_down.reshape(n, units, depth)
    pad = -owned % 8
    packed = jnp.pad(gates.T.reshape(n, owned, tokens), ((0, 0), (0, pad), (0, 0)))
    rows, got, w1, wd, w2 = gather(
        n, jnp.stack([routed, normed]), packed, gu, dn, expert_gate, expert_up, expert_down
    )
    scale = got[:, :owned].transpose(0, 2, 1).reshape(n * tokens, owned)
    sums = jnp.dot(rows[0], w1, preferred_element_type=jnp.float32)
    dense = jnp.dot(rows[1], wd, preferred_element_type=jnp.float32)
    acts = []
    for j in range(owned):
        gate = sums[:, 2 * j * share : (2 * j + 1) * share]
        up = sums[:, (2 * j + 1) * share : (2 * j + 2) * share]
        acts.append((jax.nn.silu(gate) * up * scale[:, j : j + 1]).astype(bf16))
    acts.append((jax.nn.silu(dense[:, :units]) * dense[:, units:]).astype(bf16))
    part = jnp.dot(jnp.concatenate(acts, axis=1), w2, preferred_element_type=jnp.float32)
    return reduce_sum(n, part.astype(bf16))


def own_gates(expert_ids, gate_values, experts_all):
    hit = expert_ids[:, :, None] == jnp.arange(experts_all, dtype=jnp.int32)[None, None, :]
    return jnp.sum(jnp.where(hit, gate_values[:, :, None], 0.0), axis=1)


def normalize(current, norm_gain):
    width = current.shape[1]
    wide = current.astype(jnp.float32)
    total = lax.psum(jnp.sum(wide * wide, axis=1, keepdims=True), "hidden")
    mean_square = total / norm_gain.shape[0]
    gain = lax.dynamic_slice_in_dim(norm_gain, lax.axis_index("hidden") * width, width)
    return (wide * gain[None, :] / jnp.sqrt(mean_square + 1e-06)).astype(jnp.bfloat16)


def swiglu(rows, gate, up):
    gate_sum = jnp.dot(rows, gate, preferred_element_type=jnp.float32)
    up_sum = jnp.dot(rows, up, preferred_element_type=jnp.float32)
    return jax.nn.silu(gate_sum) * up_sum


def local(
    current,
    previous,
    expert_ids,
    gate_values,
    norm_gain,
    expert_gate,
    expert_up,
    expert_down,
    dense_gate,
    dense_up,
    dense_down,
):
    owned = expert_gate.shape[0]
    owners = lax.axis_size("expert")
    bf16 = jnp.bfloat16
    routed = previous.astype(bf16)
    normed = normalize(current, norm_gain)
    gates = own_gates(expert_ids, gate_values, owned * owners)
    share, units = expert_gate.shape[2] // 2, dense_gate.shape[1] // owners
    if kernel_fits(*routed.shape, share, dense_gate.shape[0], units):
        return by_kernels(
            routed, normed, gates, expert_gate, expert_up, expert_down, dense_gate, dense_up, dense_down
        )
    swap = lambda w, axis, cut, join: lax.all_to_all(w, axis, split_axis=cut, concat_axis=join, tiled=True)
    wg = swap(expert_gate, "hidden", 2, 1)
    wu = swap(expert_up, "hidden", 2, 1)
    wd = swap(expert_down, "hidden", 1, 2)
    both = lax.all_gather(jnp.stack([routed, normed]), "expert", axis=1, tiled=True)
    both = lax.all_gather(both, "hidden", axis=2, tiled=True)
    mine = swap(gates, "expert", 1, 0)
    dg = swap(dense_gate, "expert", 1, 0)
    du = swap(dense_up, "expert", 1, 0)
    dd = swap(dense_down, "expert", 0, 1)
    acts = [
        (swiglu(both[0], wg[j], wu[j]) * mine[:, j : j + 1]).astype(bf16) for j in range(owned)
    ]
    acts.append(swiglu(both[1], dg, du).astype(bf16))
    downs = [wd[j] for j in range(owned)] + [dd]
    total = jnp.dot(
        jnp.concatenate(acts, axis=1), jnp.concatenate(downs, axis=0), preferred_element_type=jnp.float32
    ).astype(bf16)
    half = lax.psum_scatter(total, "hidden", scatter_dimension=1, tiled=True)
    return lax.psum_scatter(half, "expert", scatter_dimension=0, tiled=True)


def solution(mesh):
    placed = (
        P(("groups", "expert"), "hidden"),
        P(("groups", "expert"), "hidden"),
        P(("groups", "expert"), None),
        P(("groups", "expert"), None),
        P(),
        P("expert", "hidden", None),
        P("expert", "hidden", None),
        P("expert", None, "hidden"),
        P("expert", "hidden"),
        P("expert", "hidden"),
        P("hidden", "expert"),
    )
    return jax.shard_map(
        local,
        mesh=mesh,
        in_specs=placed,
        out_specs=P(("groups", "expert"), "hidden"),
        check_vma=False,
    )
```

```python
import functools

import jax
import jax.numpy as jnp
from jax import lax
from jax.experimental import pallas as pl
from jax.experimental.pallas import tpu as pltpu
from jax.sharding import PartitionSpec as P

MESH = pl.DeviceIdType.MESH


def ring_place(index, n):
    odd = lax.rem(index, 2)
    level = lax.div(index, 2)
    return (1 - odd) * level + odd * (n - 1 - level)


def ring_index(place, n):
    place = lax.rem(place + 2 * n, n)
    back = lax.div(place, n // 2)
    return (1 - back) * 2 * place + back * (2 * (n - 1 - place) + 1)


def rows_of(index, size):
    return pl.ds(pl.multiple_of(index * size, size), size)


def greet(peers):
    barrier = pltpu.get_barrier_semaphore()
    for peer in peers:
        pl.semaphore_signal(barrier, inc=1, device_id=peer, device_id_type=MESH)
    pl.semaphore_wait(barrier, len(peers))


def remote(src, dst, send, recv, peer):
    return pltpu.make_async_remote_copy(
        src_ref=src, dst_ref=dst, send_sem=send, recv_sem=recv, device_id=peer, device_id_type=MESH
    )


def gather_kernel(
    n, tok, gates, gu, dn, eg, eu, ed, all_tok, all_gates, w1, wd, w2,
    ring_s, ring_r, core_s, core_r, exp_s, exp_r, push_s, push_r, fwd_s, fwd_r, here,
):
    me, h, g = lax.axis_index("expert"), lax.axis_index("hidden"), lax.axis_index("groups")
    kinds, tokens, width = tok.shape
    owned, _, hidden_units = eg.shape
    share = hidden_units // 2
    depth, units = gu.shape[1], dn.shape[1]
    half = n // 2
    place = ring_place(me, n)
    right, left = {"expert": ring_index(place + 1, n)}, {"expert": ring_index(place - 1, n)}
    mate, twin = {"hidden": 1 - h}, {"groups": 1 - g}
    greet([{"expert": lax.rem(me + d, n)} for d in range(1, n)] + [mate, twin])
    pending = []
    mine = pl.ds(pl.multiple_of(h * width, width), width)

    def start(copy):
        copy.start()
        pending.append(copy)

    def block(t, origin, lo, size):
        rows = pl.ds(pl.multiple_of(origin * tokens + lo, size), size)
        return all_tok.at[t, rows, mine]

    def span(step, way):
        if step < half:
            return 0, tokens
        return way * (tokens // 2), tokens // 2

    def hop(t, step, way):
        origin = ring_index(place - (step - 1) if way == 0 else place + (step - 1), n)
        lo, size = span(step, way)
        src = tok.at[t, pl.ds(lo, size)] if step == 1 else block(t, origin, lo, size)
        k = (t * 2 + way) * half + step - 1
        return remote(src, block(t, origin, lo, size), ring_s.at[k], ring_r.at[k], right if way == 0 else left)

    def to_mate(t, origin, lo, size, k, src=None):
        view = block(t, origin, lo, size)
        k = t * (n + 1) + k
        start(remote(view if src is None else src, view, core_s.at[k], core_r.at[k], mate))

    for t in range(kinds):
        for way in range(2):
            start(hop(t, 1, way))
    locals_ = []

    def keep(src, dst):
        copy = pltpu.make_async_copy(src, dst, here.at[len(locals_)])
        copy.start()
        locals_.append(copy)

    pushes = []
    for d in range(1, n):
        to = lax.rem(me + d, n)
        peer = {"expert": to}
        rows = pl.ds(pl.multiple_of(g * (depth // 2), depth // 2), depth // 2)
        into = pl.ds(pl.multiple_of(me * depth + g * (depth // 2), depth // 2), depth // 2)
        a = remote(gu.at[to, rows], wd.at[into], push_s.at[3 * d], push_r.at[3 * d], peer)
        rows = pl.ds(pl.multiple_of(g * (units // 2), units // 2), units // 2)
        into = pl.ds(pl.multiple_of(owned * share + g * (units // 2), 16), units // 2)
        b = remote(
            dn.at[to, rows], w2.at[into, rows_of(me, depth)], push_s.at[3 * d + 1], push_r.at[3 * d + 1], peer
        )
        c = remote(gates.at[to], all_gates.at[me], push_s.at[3 * d + 2], push_r.at[3 * d + 2], peer)
        for copy in (a, b, c):
            copy.start()
        pushes.append((a, b, c))
    swaps = []

    def swap_expert(j):
        away = pl.ds(pl.multiple_of((1 - h) * share, 128), share)
        stay = pl.ds(pl.multiple_of(h * share, 128), share)
        for i, w in enumerate((eg, eu)):
            spot = w1.at[rows_of(h, width), pl.ds((2 * j + i) * share, share)]
            k = 3 * j + i
            swaps.append(remote(w.at[j, :, away], spot, exp_s.at[k], exp_r.at[k], mate))
            swaps[-1].start()
            keep(w.at[j, :, stay], spot)
        spot = w2.at[pl.ds(j * share, share), mine]
        away = pl.ds(pl.multiple_of((1 - h) * share, 16), share)
        stay = pl.ds(pl.multiple_of(h * share, 16), share)
        swaps.append(remote(ed.at[j, away], spot, exp_s.at[3 * j + 2], exp_r.at[3 * j + 2], mate))
        swaps[-1].start()
        keep(ed.at[j, stay], spot)

    for t in range(kinds):
        to_mate(t, me, 0, tokens, 0, tok.at[t])
        keep(tok.at[t], block(t, me, 0, tokens))
    keep(gu.at[me], wd.at[rows_of(me, depth)])
    keep(dn.at[me], w2.at[pl.ds(owned * share, units), rows_of(me, depth)])
    keep(gates.at[me], all_gates.at[me])

    forwards = []

    def pass_on(d):
        for copy in pushes[d - 1]:
            copy.wait_recv()
        source = lax.rem(me - d + n, n)
        into = pl.ds(pl.multiple_of(source * depth + g * (depth // 2), depth // 2), depth // 2)
        a = remote(wd.at[into], wd.at[into], fwd_s.at[2 * d], fwd_r.at[2 * d], twin)
        into = pl.ds(pl.multiple_of(owned * share + g * (units // 2), 16), units // 2)
        spot = w2.at[into, rows_of(source, depth)]
        b = remote(spot, spot, fwd_s.at[2 * d + 1], fwd_r.at[2 * d + 1], twin)
        for copy in (a, b):
            copy.start()
            forwards.append(copy)

    late = list(range(1, n))
    for step in range(1, half + 1):
        for t in range(kinds):
            for way in range(2):
                hop(t, step, way).wait_recv()
                origin = ring_index(place - step if way == 0 else place + step, n)
                lo, size = span(step, way)
                if step < half:
                    start(hop(t, step + 1, way))
                to_mate(t, origin, lo, size, 2 * step - 1 + way)
        for j in range(owned):
            if min(j + 1, half - 1) == step:
                swap_expert(j)
        if step == half - 1:
            for _ in range(half - 1):
                pass_on(late.pop(0))
    while late:
        pass_on(late.pop(0))
    for copy in pending:
        copy.wait_send()
    for t in range(kinds):
        for k in range(n + 1):
            step, way = (k + 1) // 2, (k + 1) % 2
            lo, size = (0, tokens) if k == 0 else span(step, way)
            origin = ring_index(place if k == 0 else (place - step if way == 0 else place + step), n)
            theirs = pl.ds(pl.multiple_of((1 - h) * width, width), width)
            rows = pl.ds(pl.multiple_of(origin * tokens + lo, size), size)
            view = all_tok.at[t, rows, theirs]
            remote(view, view, core_s.at[t * (n + 1) + k], core_r.at[t * (n + 1) + k], mate).wait_recv()
    for copy in swaps + forwards:
        copy.wait()
    for group in pushes:
        for copy in group:
            copy.wait_send()
    for copy in locals_:
        copy.wait()


def gather(n, tok, gates, gu, dn, eg, eu, ed):
    kinds, tokens, width = tok.shape
    owned, _, hidden_units = eg.shape
    depth, units = gu.shape[1], dn.shape[1]
    share = hidden_units // 2
    dma = lambda count: pltpu.SemaphoreType.DMA((count,))
    shape = jax.ShapeDtypeStruct
    bf16 = jnp.bfloat16
    return pl.pallas_call(
        functools.partial(gather_kernel, n),
        out_shape=(
            shape((kinds, n * tokens, 2 * width), bf16),
            shape(gates.shape, gates.dtype),
            shape((2 * width, 2 * owned * share), bf16),
            shape((n * depth, gu.shape[2]), bf16),
            shape((owned * share + units, 2 * width), bf16),
        ),
        in_specs=[pl.BlockSpec(memory_space=pl.ANY)] * 7,
        out_specs=[pl.BlockSpec(memory_space=pltpu.VMEM)] * 5,
        scratch_shapes=[dma(kinds * n)] * 2
        + [dma(kinds * (n + 1))] * 2
        + [dma(3 * owned)] * 2
        + [dma(3 * n)] * 2
        + [dma(2 * n)] * 2
        + [dma(3 * owned + kinds + 3)],
        compiler_params=pltpu.CompilerParams(
            collective_id=0, has_side_effects=True, vmem_limit_bytes=48 * 2**20
        ),
    )(tok, gates, gu, dn, eg, eu, ed)


def reduce_kernel(n, part, out, core, sent, got, core_s, core_r, ring_s, ring_r):
    me, h = lax.axis_index("expert"), lax.axis_index("hidden")
    tokens, width = out.shape
    half = n // 2
    place = ring_place(me, n)
    right, left = {"expert": ring_index(place + 1, n)}, {"expert": ring_index(place - 1, n)}
    mate = {"hidden": 1 - h}
    greet([right, left, mate])
    mine = pl.ds(pl.multiple_of(h * width, width), width)
    theirs = pl.ds(pl.multiple_of((1 - h) * width, width), width)
    order = [half]
    for d in range(half - 1, 0, -1):
        order += [d, -d]
    order.append(0)
    trades = {}
    for k, d in enumerate(order):
        rows = rows_of(ring_index(place + d, n), tokens)
        trades[d] = remote(part.at[rows, theirs], core.at[rows], core_s.at[k], core_r.at[k], mate)
        trades[d].start()

    def own(d):
        trades[d].wait_recv()
        rows = rows_of(ring_index(place + d, n), tokens)
        return part[rows, mine].astype(jnp.float32) + core[rows].astype(jnp.float32)

    def view(buffer, step, way):
        k = way * half + step - 1
        if step == 1:
            return buffer.at[k, pl.ds(way * (tokens // 2), tokens // 2)]
        return buffer.at[k]

    def hop(step, way):
        k = way * half + step - 1
        return remote(
            view(sent, step, way), view(got, step, way), ring_s.at[k], ring_r.at[k], right if way == 0 else left
        )

    far = own(half).astype(jnp.bfloat16)
    hops = []
    for step in range(1, half + 1):
        for way in range(2):
            k = way * half + step - 1
            if step == 1:
                lo = way * (tokens // 2)
                sent[k, pl.ds(lo, tokens // 2)] = far[lo : lo + tokens // 2]
            else:
                d = half + 1 - step
                value = own(d if way == 0 else -d)
                hop(step - 1, way).wait_recv()
                if step == 2:
                    lo = way * (tokens // 2)
                    other = tokens // 2 - lo
                    cut = slice(lo, lo + tokens // 2)
                    add = got[k - 1, pl.ds(lo, tokens // 2)].astype(jnp.float32)
                    sent[k, pl.ds(lo, tokens // 2)] = (value[cut] + add).astype(jnp.bfloat16)
                    sent[k, pl.ds(other, tokens // 2)] = value[other : other + tokens // 2].astype(jnp.bfloat16)
                else:
                    sent[k] = (value + got[k - 1].astype(jnp.float32)).astype(jnp.bfloat16)
            copy = hop(step, way)
            copy.start()
            hops.append(copy)
    value = own(0)
    for way in range(2):
        hop(half, way).wait_recv()
        value = value + got[way * half + half - 1].astype(jnp.float32)
    out[...] = value.astype(jnp.bfloat16)
    for copy in hops:
        copy.wait_send()
    for copy in trades.values():
        copy.wait_send()


def reduce_sum(n, part):
    tokens, width = part.shape[0] // n, part.shape[1] // 2
    bf16 = jnp.bfloat16
    dma = lambda count: pltpu.SemaphoreType.DMA((count,))
    return pl.pallas_call(
        functools.partial(reduce_kernel, n),
        out_shape=jax.ShapeDtypeStruct((tokens, width), bf16),
        in_specs=[pl.BlockSpec(memory_space=pltpu.VMEM)],
        out_specs=pl.BlockSpec(memory_space=pltpu.VMEM),
        scratch_shapes=[
            pltpu.VMEM((n * tokens, width), bf16),
            pltpu.VMEM((n, tokens, width), bf16),
            pltpu.VMEM((n, tokens, width), bf16),
            dma(n), dma(n), dma(n), dma(n),
        ],
        compiler_params=pltpu.CompilerParams(
            collective_id=1, has_side_effects=True, vmem_limit_bytes=40 * 2**20
        ),
    )(part)


def kernel_fits(tokens, width, share, depth, units):
    pairs = lax.axis_size("hidden") == 2 and lax.axis_size("groups") == 2
    even = lax.axis_size("expert") % 2 == 0 and lax.axis_size("expert") >= 4
    aligned = tokens % 128 == 0 and width % 128 == 0 and share % 128 == 0
    return pairs and even and aligned and depth % 128 == 0 and units % 32 == 0


def by_kernels(routed, normed, gates, expert_gate, expert_up, expert_down, dense_gate, dense_up, dense_down):
    n = lax.axis_size("expert")
    tokens = routed.shape[0]
    owned, _, hidden_units = expert_gate.shape
    share = hidden_units // 2
    depth, spread = dense_gate.shape
    units = spread // n
    bf16 = jnp.bfloat16
    cut = lambda w: w.reshape(depth, n, units).transpose(1, 0, 2)
    gu = jnp.concatenate([cut(dense_gate), cut(dense_up)], axis=2)
    dn = dense_down.reshape(n, units, depth)
    pad = -owned % 8
    packed = jnp.pad(gates.T.reshape(n, owned, tokens), ((0, 0), (0, pad), (0, 0)))
    rows, got, w1, wd, w2 = gather(
        n, jnp.stack([routed, normed]), packed, gu, dn, expert_gate, expert_up, expert_down
    )
    scale = got[:, :owned].transpose(0, 2, 1).reshape(n * tokens, owned)
    sums = jnp.dot(rows[0], w1, preferred_element_type=jnp.float32)
    dense = jnp.dot(rows[1], wd, preferred_element_type=jnp.float32)
    acts = []
    for j in range(owned):
        gate = sums[:, 2 * j * share : (2 * j + 1) * share]
        up = sums[:, (2 * j + 1) * share : (2 * j + 2) * share]
        acts.append((jax.nn.silu(gate) * up * scale[:, j : j + 1]).astype(bf16))
    acts.append((jax.nn.silu(dense[:, :units]) * dense[:, units:]).astype(bf16))
    part = jnp.dot(jnp.concatenate(acts, axis=1), w2, preferred_element_type=jnp.float32)
    return reduce_sum(n, part.astype(bf16))


def own_gates(expert_ids, gate_values, experts_all):
    hit = expert_ids[:, :, None] == jnp.arange(experts_all, dtype=jnp.int32)[None, None, :]
    return jnp.sum(jnp.where(hit, gate_values[:, :, None], 0.0), axis=1)


def normalize(current, norm_gain):
    width = current.shape[1]
    wide = current.astype(jnp.float32)
    total = lax.psum(jnp.sum(wide * wide, axis=1, keepdims=True), "hidden")
    mean_square = total / norm_gain.shape[0]
    gain = lax.dynamic_slice_in_dim(norm_gain, lax.axis_index("hidden") * width, width)
    return (wide * gain[None, :] / jnp.sqrt(mean_square + 1e-06)).astype(jnp.bfloat16)


def swiglu(rows, gate, up):
    gate_sum = jnp.dot(rows, gate, preferred_element_type=jnp.float32)
    up_sum = jnp.dot(rows, up, preferred_element_type=jnp.float32)
    return jax.nn.silu(gate_sum) * up_sum


def local(
    current,
    previous,
    expert_ids,
    gate_values,
    norm_gain,
    expert_gate,
    expert_up,
    expert_down,
    dense_gate,
    dense_up,
    dense_down,
):
    owned = expert_gate.shape[0]
    owners = lax.axis_size("expert")
    bf16 = jnp.bfloat16
    routed = previous.astype(bf16)
    normed = normalize(current, norm_gain)
    gates = own_gates(expert_ids, gate_values, owned * owners)
    share, units = expert_gate.shape[2] // 2, dense_gate.shape[1] // owners
    if kernel_fits(*routed.shape, share, dense_gate.shape[0], units):
        return by_kernels(
            routed, normed, gates, expert_gate, expert_up, expert_down, dense_gate, dense_up, dense_down
        )
    swap = lambda w, axis, cut, join: lax.all_to_all(w, axis, split_axis=cut, concat_axis=join, tiled=True)
    wg = swap(expert_gate, "hidden", 2, 1)
    wu = swap(expert_up, "hidden", 2, 1)
    wd = swap(expert_down, "hidden", 1, 2)
    both = lax.all_gather(jnp.stack([routed, normed]), "expert", axis=1, tiled=True)
    both = lax.all_gather(both, "hidden", axis=2, tiled=True)
    mine = swap(gates, "expert", 1, 0)
    dg = swap(dense_gate, "expert", 1, 0)
    du = swap(dense_up, "expert", 1, 0)
    dd = swap(dense_down, "expert", 0, 1)
    acts = [
        (swiglu(both[0], wg[j], wu[j]) * mine[:, j : j + 1]).astype(bf16) for j in range(owned)
    ]
    acts.append(swiglu(both[1], dg, du).astype(bf16))
    downs = [wd[j] for j in range(owned)] + [dd]
    total = jnp.dot(
        jnp.concatenate(acts, axis=1), jnp.concatenate(downs, axis=0), preferred_element_type=jnp.float32
    ).astype(bf16)
    half = lax.psum_scatter(total, "hidden", scatter_dimension=1, tiled=True)
    return lax.psum_scatter(half, "expert", scatter_dimension=0, tiled=True)


def solution(mesh):
    placed = (
        P(("groups", "expert"), "hidden"),
        P(("groups", "expert"), "hidden"),
        P(("groups", "expert"), None),
        P(("groups", "expert"), None),
        P(),
        P("expert", "hidden", None),
        P("expert", "hidden", None),
        P("expert", None, "hidden"),
        P("expert", "hidden"),
        P("expert", "hidden"),
        P("hidden", "expert"),
    )
    return jax.shard_map(
        local,
        mesh=mesh,
        in_specs=placed,
        out_specs=P(("groups", "expert"), "hidden"),
        check_vma=False,
    )
```

```python
import functools

import jax
import jax.numpy as jnp
from jax import lax
from jax.experimental import pallas as pl
from jax.experimental.pallas import tpu as pltpu
from jax.sharding import PartitionSpec as P

MESH = pl.DeviceIdType.MESH


def ring_place(index, n):
    odd = lax.rem(index, 2)
    level = lax.div(index, 2)
    return (1 - odd) * level + odd * (n - 1 - level)


def ring_index(place, n):
    place = lax.rem(place + 2 * n, n)
    back = lax.div(place, n // 2)
    return (1 - back) * 2 * place + back * (2 * (n - 1 - place) + 1)


def rows_of(index, size):
    return pl.ds(pl.multiple_of(index * size, size), size)


def greet(peers):
    barrier = pltpu.get_barrier_semaphore()
    for peer in peers:
        pl.semaphore_signal(barrier, inc=1, device_id=peer, device_id_type=MESH)
    pl.semaphore_wait(barrier, len(peers))


def remote(src, dst, send, recv, peer):
    return pltpu.make_async_remote_copy(
        src_ref=src, dst_ref=dst, send_sem=send, recv_sem=recv, device_id=peer, device_id_type=MESH
    )


def gather_kernel(
    n, tok, gates, gu, dn, eg, eu, ed, acts, w2, all_tok, all_gates, w1, wd,
    ring_s, ring_r, core_s, core_r, exp_s, exp_r, push_s, push_r, fwd_s, fwd_r, here,
):
    me, h, g = lax.axis_index("expert"), lax.axis_index("hidden"), lax.axis_index("groups")
    kinds, tokens, width = tok.shape
    owned, _, hidden_units = eg.shape
    share = hidden_units // 2
    depth, units = gu.shape[1], dn.shape[1]
    half = n // 2
    place = ring_place(me, n)
    right, left = {"expert": ring_index(place + 1, n)}, {"expert": ring_index(place - 1, n)}
    mate, twin = {"hidden": 1 - h}, {"groups": 1 - g}
    greet([{"expert": lax.rem(me + d, n)} for d in range(1, n)] + [mate, twin])
    pending = []
    mine = pl.ds(pl.multiple_of(h * width, width), width)

    def start(copy):
        copy.start()
        pending.append(copy)

    def block(t, origin, lo, size):
        rows = pl.ds(pl.multiple_of(origin * tokens + lo, size), size)
        return all_tok.at[t, rows, mine]

    def span(step, way):
        if step < half:
            return 0, tokens
        return way * (tokens // 2), tokens // 2

    def hop(t, step, way):
        origin = ring_index(place - (step - 1) if way == 0 else place + (step - 1), n)
        lo, size = span(step, way)
        src = tok.at[t, pl.ds(lo, size)] if step == 1 else block(t, origin, lo, size)
        k = (t * 2 + way) * half + step - 1
        return remote(src, block(t, origin, lo, size), ring_s.at[k], ring_r.at[k], right if way == 0 else left)

    def to_mate(t, origin, lo, size, k, src=None):
        view = block(t, origin, lo, size)
        k = t * (n + 1) + k
        start(remote(view if src is None else src, view, core_s.at[k], core_r.at[k], mate))

    for t in range(kinds):
        for way in range(2):
            start(hop(t, 1, way))
    locals_ = []

    def keep(src, dst):
        copy = pltpu.make_async_copy(src, dst, here.at[len(locals_)])
        copy.start()
        locals_.append(copy)

    pushes, gate_copies = [], []
    for d in range(1, n):
        to = lax.rem(me + d, n)
        peer = {"expert": to}
        rows = pl.ds(pl.multiple_of(g * (depth // 2), depth // 2), depth // 2)
        into = pl.ds(pl.multiple_of(me * depth + g * (depth // 2), depth // 2), depth // 2)
        a = remote(gu.at[to, rows], wd.at[into], push_s.at[3 * d], push_r.at[3 * d], peer)
        rows = pl.ds(pl.multiple_of(g * (units // 2), units // 2), units // 2)
        into = pl.ds(pl.multiple_of(owned * share + g * (units // 2), 16), units // 2)
        b = remote(
            dn.at[to, rows], w2.at[into, rows_of(me, depth)], push_s.at[3 * d + 1], push_r.at[3 * d + 1], peer
        )
        c = remote(gates.at[to], all_gates.at[me], push_s.at[3 * d + 2], push_r.at[3 * d + 2], peer)
        for copy in (c, a, b):
            copy.start()
        pushes.append((a, b))
        gate_copies.append(c)
    swaps = []

    def swap_expert(j):
        away = pl.ds(pl.multiple_of((1 - h) * share, 128), share)
        stay = pl.ds(pl.multiple_of(h * share, 128), share)
        for i, w in enumerate((eg, eu)):
            spot = w1.at[rows_of(h, width), pl.ds((2 * j + i) * share, share)]
            k = 3 * j + i
            swaps.append(remote(w.at[j, :, away], spot, exp_s.at[k], exp_r.at[k], mate))
            swaps[-1].start()
            keep(w.at[j, :, stay], spot)
        spot = w2.at[pl.ds(j * share, share), mine]
        away = pl.ds(pl.multiple_of((1 - h) * share, 16), share)
        stay = pl.ds(pl.multiple_of(h * share, 16), share)
        swaps.append(remote(ed.at[j, away], spot, exp_s.at[3 * j + 2], exp_r.at[3 * j + 2], mate))
        swaps[-1].start()
        keep(ed.at[j, stay], spot)

    for t in range(kinds):
        to_mate(t, me, 0, tokens, 0, tok.at[t])
        keep(tok.at[t], block(t, me, 0, tokens))
    keep(gu.at[me], wd.at[rows_of(me, depth)])
    keep(dn.at[me], w2.at[pl.ds(owned * share, units), rows_of(me, depth)])
    keep(gates.at[me], all_gates.at[me])

    for j in range(owned):
        swap_expert(j)
    forwards = []

    def from_mate(t, k):
        step, way = (k + 1) // 2, (k + 1) % 2
        lo, size = (0, tokens) if k == 0 else span(step, way)
        origin = ring_index(place if k == 0 else (place - step if way == 0 else place + step), n)
        theirs = pl.ds(pl.multiple_of((1 - h) * width, width), width)
        rows = pl.ds(pl.multiple_of(origin * tokens + lo, size), size)
        view = all_tok.at[t, rows, theirs]
        k = t * (n + 1) + k
        remote(view, view, core_s.at[k], core_r.at[k], mate).wait_recv()

    def swish(gate, up):
        return gate / (1.0 + jnp.exp(-gate)) * up

    def experts(first, count):
        def body(i, carry):
            origin = ring_index(place + first + i, n)
            rows = rows_of(origin, tokens)
            sums = jnp.dot(all_tok[0, rows], w1[...], preferred_element_type=jnp.float32)
            scale = all_gates[origin].T
            for j in range(owned):
                gate = sums[:, 2 * j * share : (2 * j + 1) * share]
                up = sums[:, (2 * j + 1) * share : (2 * j + 2) * share]
                value = swish(gate, up) * scale[:, j : j + 1]
                acts[rows, j * share : (j + 1) * share] = value.astype(jnp.bfloat16)
            return carry

        lax.fori_loop(0, count, body, 0)

    def dense():
        def body(i, carry):
            rows = rows_of(i, 2 * tokens)
            sums = jnp.dot(all_tok[1, rows], wd[...], preferred_element_type=jnp.float32)
            value = swish(sums[:, :units], sums[:, units:])
            acts[rows, owned * share : owned * share + units] = value.astype(jnp.bfloat16)
            return carry

        lax.fori_loop(0, n // 2, body, 0)

    def pass_on(d):
        for copy in pushes[d - 1]:
            copy.wait_recv()
        source = lax.rem(me - d + n, n)
        into = pl.ds(pl.multiple_of(source * depth + g * (depth // 2), depth // 2), depth // 2)
        a = remote(wd.at[into], wd.at[into], fwd_s.at[2 * d], fwd_r.at[2 * d], twin)
        into = pl.ds(pl.multiple_of(owned * share + g * (units // 2), 16), units // 2)
        spot = w2.at[into, rows_of(source, depth)]
        b = remote(spot, spot, fwd_s.at[2 * d + 1], fwd_r.at[2 * d + 1], twin)
        for copy in (a, b):
            copy.start()
            forwards.append(copy)

    late = list(range(1, n))
    for step in range(1, half + 1):
        for t in range(kinds):
            for way in range(2):
                hop(t, step, way).wait_recv()
                origin = ring_index(place - step if way == 0 else place + step, n)
                lo, size = span(step, way)
                if step < half:
                    start(hop(t, step + 1, way))
                to_mate(t, origin, lo, size, 2 * step - 1 + way)
        if step == half - 1:
            for _ in range(half - 1):
                pass_on(late.pop(0))
            for copy in swaps:
                copy.wait()
            for copy in locals_:
                copy.wait()
            for copy in gate_copies:
                copy.wait()
            for k in range(2 * half - 3):
                from_mate(0, k)
            experts(2 - half, 2 * half - 3)
    while late:
        pass_on(late.pop(0))
    for k in range(2 * half - 3, n + 1):
        from_mate(0, k)
    experts(half - 1, 3)
    for k in range(n + 1):
        from_mate(1, k)
    for copy in forwards:
        copy.wait()
    dense()
    for copy in pending:
        copy.wait_send()
    for group in pushes:
        for copy in group:
            copy.wait_send()


def gather(n, tok, gates, gu, dn, eg, eu, ed):
    kinds, tokens, width = tok.shape
    owned, _, hidden_units = eg.shape
    depth, units = gu.shape[1], dn.shape[1]
    share = hidden_units // 2
    dma = lambda count: pltpu.SemaphoreType.DMA((count,))
    shape = jax.ShapeDtypeStruct
    bf16 = jnp.bfloat16
    return pl.pallas_call(
        functools.partial(gather_kernel, n),
        out_shape=(
            shape((n * tokens, owned * share + units), bf16),
            shape((owned * share + units, 2 * width), bf16),
        ),
        in_specs=[pl.BlockSpec(memory_space=pl.ANY)] * 7,
        out_specs=[pl.BlockSpec(memory_space=pltpu.VMEM)] * 2,
        scratch_shapes=[
            pltpu.VMEM((kinds, n * tokens, 2 * width), bf16),
            pltpu.VMEM(gates.shape, gates.dtype),
            pltpu.VMEM((2 * width, 2 * owned * share), bf16),
            pltpu.VMEM((n * depth, gu.shape[2]), bf16),
        ]
        + [dma(kinds * n)] * 2
        + [dma(kinds * (n + 1))] * 2
        + [dma(3 * owned)] * 2
        + [dma(3 * n)] * 2
        + [dma(2 * n)] * 2
        + [dma(3 * owned + kinds + 3)],
        compiler_params=pltpu.CompilerParams(
            collective_id=0, has_side_effects=True, vmem_limit_bytes=48 * 2**20
        ),
    )(tok, gates, gu, dn, eg, eu, ed)


def reduce_kernel(n, part, out, core, sent, got, core_s, core_r, ring_s, ring_r):
    me, h = lax.axis_index("expert"), lax.axis_index("hidden")
    tokens, width = out.shape
    half = n // 2
    place = ring_place(me, n)
    right, left = {"expert": ring_index(place + 1, n)}, {"expert": ring_index(place - 1, n)}
    mate = {"hidden": 1 - h}
    greet([right, left, mate])
    mine = pl.ds(pl.multiple_of(h * width, width), width)
    theirs = pl.ds(pl.multiple_of((1 - h) * width, width), width)
    order = [half]
    for d in range(half - 1, 0, -1):
        order += [d, -d]
    order.append(0)
    trades = {}
    for k, d in enumerate(order):
        rows = rows_of(ring_index(place + d, n), tokens)
        trades[d] = remote(part.at[rows, theirs], core.at[rows], core_s.at[k], core_r.at[k], mate)
        trades[d].start()

    def own(d):
        trades[d].wait_recv()
        rows = rows_of(ring_index(place + d, n), tokens)
        return part[rows, mine].astype(jnp.float32) + core[rows].astype(jnp.float32)

    def view(buffer, step, way):
        k = way * half + step - 1
        if step == 1:
            return buffer.at[k, pl.ds(way * (tokens // 2), tokens // 2)]
        return buffer.at[k]

    def hop(step, way):
        k = way * half + step - 1
        return remote(
            view(sent, step, way), view(got, step, way), ring_s.at[k], ring_r.at[k], right if way == 0 else left
        )

    far = own(half).astype(jnp.bfloat16)
    hops = []
    for step in range(1, half + 1):
        for way in range(2):
            k = way * half + step - 1
            if step == 1:
                lo = way * (tokens // 2)
                sent[k, pl.ds(lo, tokens // 2)] = far[lo : lo + tokens // 2]
            else:
                d = half + 1 - step
                value = own(d if way == 0 else -d)
                hop(step - 1, way).wait_recv()
                if step == 2:
                    lo = way * (tokens // 2)
                    other = tokens // 2 - lo
                    cut = slice(lo, lo + tokens // 2)
                    add = got[k - 1, pl.ds(lo, tokens // 2)].astype(jnp.float32)
                    sent[k, pl.ds(lo, tokens // 2)] = (value[cut] + add).astype(jnp.bfloat16)
                    sent[k, pl.ds(other, tokens // 2)] = value[other : other + tokens // 2].astype(jnp.bfloat16)
                else:
                    sent[k] = (value + got[k - 1].astype(jnp.float32)).astype(jnp.bfloat16)
            copy = hop(step, way)
            copy.start()
            hops.append(copy)
    value = own(0)
    for way in range(2):
        hop(half, way).wait_recv()
        value = value + got[way * half + half - 1].astype(jnp.float32)
    out[...] = value.astype(jnp.bfloat16)
    for copy in hops:
        copy.wait_send()
    for copy in trades.values():
        copy.wait_send()


def reduce_sum(n, part):
    tokens, width = part.shape[0] // n, part.shape[1] // 2
    bf16 = jnp.bfloat16
    dma = lambda count: pltpu.SemaphoreType.DMA((count,))
    return pl.pallas_call(
        functools.partial(reduce_kernel, n),
        out_shape=jax.ShapeDtypeStruct((tokens, width), bf16),
        in_specs=[pl.BlockSpec(memory_space=pltpu.VMEM)],
        out_specs=pl.BlockSpec(memory_space=pltpu.VMEM),
        scratch_shapes=[
            pltpu.VMEM((n * tokens, width), bf16),
            pltpu.VMEM((n, tokens, width), bf16),
            pltpu.VMEM((n, tokens, width), bf16),
            dma(n), dma(n), dma(n), dma(n),
        ],
        compiler_params=pltpu.CompilerParams(
            collective_id=1, has_side_effects=True, vmem_limit_bytes=40 * 2**20
        ),
    )(part)


def kernel_fits(tokens, width, share, depth, units):
    pairs = lax.axis_size("hidden") == 2 and lax.axis_size("groups") == 2
    even = lax.axis_size("expert") % 2 == 0 and lax.axis_size("expert") >= 4
    aligned = tokens % 128 == 0 and width % 128 == 0 and share % 128 == 0
    return pairs and even and aligned and depth % 128 == 0 and units % 32 == 0


def by_kernels(routed, normed, gates, expert_gate, expert_up, expert_down, dense_gate, dense_up, dense_down):
    n = lax.axis_size("expert")
    tokens = routed.shape[0]
    owned, _, hidden_units = expert_gate.shape
    share = hidden_units // 2
    depth, spread = dense_gate.shape
    units = spread // n
    bf16 = jnp.bfloat16
    cut = lambda w: w.reshape(depth, n, units).transpose(1, 0, 2)
    gu = jnp.concatenate([cut(dense_gate), cut(dense_up)], axis=2)
    dn = dense_down.reshape(n, units, depth)
    pad = -owned % 8
    packed = jnp.pad(gates.T.reshape(n, owned, tokens), ((0, 0), (0, pad), (0, 0)))
    acts, w2 = gather(
        n, jnp.stack([routed, normed]), packed, gu, dn, expert_gate, expert_up, expert_down
    )
    part = jnp.dot(acts, w2, preferred_element_type=jnp.float32)
    return reduce_sum(n, part.astype(bf16))


def own_gates(expert_ids, gate_values, experts_all):
    hit = expert_ids[:, :, None] == jnp.arange(experts_all, dtype=jnp.int32)[None, None, :]
    return jnp.sum(jnp.where(hit, gate_values[:, :, None], 0.0), axis=1)


def normalize(current, norm_gain):
    width = current.shape[1]
    wide = current.astype(jnp.float32)
    total = lax.psum(jnp.sum(wide * wide, axis=1, keepdims=True), "hidden")
    mean_square = total / norm_gain.shape[0]
    gain = lax.dynamic_slice_in_dim(norm_gain, lax.axis_index("hidden") * width, width)
    return (wide * gain[None, :] / jnp.sqrt(mean_square + 1e-06)).astype(jnp.bfloat16)


def swiglu(rows, gate, up):
    gate_sum = jnp.dot(rows, gate, preferred_element_type=jnp.float32)
    up_sum = jnp.dot(rows, up, preferred_element_type=jnp.float32)
    return jax.nn.silu(gate_sum) * up_sum


def local(
    current,
    previous,
    expert_ids,
    gate_values,
    norm_gain,
    expert_gate,
    expert_up,
    expert_down,
    dense_gate,
    dense_up,
    dense_down,
):
    owned = expert_gate.shape[0]
    owners = lax.axis_size("expert")
    bf16 = jnp.bfloat16
    routed = previous.astype(bf16)
    normed = normalize(current, norm_gain)
    gates = own_gates(expert_ids, gate_values, owned * owners)
    share, units = expert_gate.shape[2] // 2, dense_gate.shape[1] // owners
    if kernel_fits(*routed.shape, share, dense_gate.shape[0], units):
        return by_kernels(
            routed, normed, gates, expert_gate, expert_up, expert_down, dense_gate, dense_up, dense_down
        )
    swap = lambda w, axis, cut, join: lax.all_to_all(w, axis, split_axis=cut, concat_axis=join, tiled=True)
    wg = swap(expert_gate, "hidden", 2, 1)
    wu = swap(expert_up, "hidden", 2, 1)
    wd = swap(expert_down, "hidden", 1, 2)
    both = lax.all_gather(jnp.stack([routed, normed]), "expert", axis=1, tiled=True)
    both = lax.all_gather(both, "hidden", axis=2, tiled=True)
    mine = swap(gates, "expert", 1, 0)
    dg = swap(dense_gate, "expert", 1, 0)
    du = swap(dense_up, "expert", 1, 0)
    dd = swap(dense_down, "expert", 0, 1)
    acts = [
        (swiglu(both[0], wg[j], wu[j]) * mine[:, j : j + 1]).astype(bf16) for j in range(owned)
    ]
    acts.append(swiglu(both[1], dg, du).astype(bf16))
    downs = [wd[j] for j in range(owned)] + [dd]
    total = jnp.dot(
        jnp.concatenate(acts, axis=1), jnp.concatenate(downs, axis=0), preferred_element_type=jnp.float32
    ).astype(bf16)
    half = lax.psum_scatter(total, "hidden", scatter_dimension=1, tiled=True)
    return lax.psum_scatter(half, "expert", scatter_dimension=0, tiled=True)


def solution(mesh):
    placed = (
        P(("groups", "expert"), "hidden"),
        P(("groups", "expert"), "hidden"),
        P(("groups", "expert"), None),
        P(("groups", "expert"), None),
        P(),
        P("expert", "hidden", None),
        P("expert", "hidden", None),
        P("expert", None, "hidden"),
        P("expert", "hidden"),
        P("expert", "hidden"),
        P("hidden", "expert"),
    )
    return jax.shard_map(
        local,
        mesh=mesh,
        in_specs=placed,
        out_specs=P(("groups", "expert"), "hidden"),
        check_vma=False,
    )
```

```python
import functools

import jax
import jax.numpy as jnp
from jax import lax
from jax.experimental import pallas as pl
from jax.experimental.pallas import tpu as pltpu
from jax.sharding import PartitionSpec as P

MESH = pl.DeviceIdType.MESH


def ring_place(index, n):
    odd = lax.rem(index, 2)
    level = lax.div(index, 2)
    return (1 - odd) * level + odd * (n - 1 - level)


def ring_index(place, n):
    place = lax.rem(place + 2 * n, n)
    back = lax.div(place, n // 2)
    return (1 - back) * 2 * place + back * (2 * (n - 1 - place) + 1)


def rows_of(index, size):
    return pl.ds(pl.multiple_of(index * size, size), size)


def greet(peers):
    barrier = pltpu.get_barrier_semaphore()
    for peer in peers:
        pl.semaphore_signal(barrier, inc=1, device_id=peer, device_id_type=MESH)
    pl.semaphore_wait(barrier, len(peers))


def remote(src, dst, send, recv, peer):
    return pltpu.make_async_remote_copy(
        src_ref=src, dst_ref=dst, send_sem=send, recv_sem=recv, device_id=peer, device_id_type=MESH
    )


def gather_kernel(
    n, tok, gates, gu, dn, eg, eu, ed, acts, w2, all_tok, all_gates, w1, wd,
    ring_s, ring_r, core_s, core_r, exp_s, exp_r, push_s, push_r, fwd_s, fwd_r, here,
):
    me, h, g = lax.axis_index("expert"), lax.axis_index("hidden"), lax.axis_index("groups")
    kinds, tokens, width = tok.shape
    owned, _, hidden_units = eg.shape
    share = hidden_units // 2
    depth, units = gu.shape[1], dn.shape[1]
    half = n // 2
    place = ring_place(me, n)
    right, left = {"expert": ring_index(place + 1, n)}, {"expert": ring_index(place - 1, n)}
    mate, twin = {"hidden": 1 - h}, {"groups": 1 - g}
    greet([{"expert": lax.rem(me + d, n)} for d in range(1, n)] + [mate, twin])
    pending = []
    mine = pl.ds(pl.multiple_of(h * width, width), width)

    def start(copy):
        copy.start()
        pending.append(copy)

    def block(t, origin, lo, size):
        rows = pl.ds(pl.multiple_of(origin * tokens + lo, size), size)
        return all_tok.at[t, rows, mine]

    def span(step, way):
        if step < half:
            return 0, tokens
        return way * (tokens // 2), tokens // 2

    def hop(t, step, way):
        origin = ring_index(place - (step - 1) if way == 0 else place + (step - 1), n)
        lo, size = span(step, way)
        src = tok.at[t, pl.ds(lo, size)] if step == 1 else block(t, origin, lo, size)
        k = (t * 2 + way) * half + step - 1
        return remote(src, block(t, origin, lo, size), ring_s.at[k], ring_r.at[k], right if way == 0 else left)

    def to_mate(t, origin, lo, size, k, src=None):
        view = block(t, origin, lo, size)
        k = t * (n + 1) + k
        start(remote(view if src is None else src, view, core_s.at[k], core_r.at[k], mate))

    for t in range(kinds):
        for way in range(2):
            start(hop(t, 1, way))
    locals_ = []

    def keep(src, dst):
        copy = pltpu.make_async_copy(src, dst, here.at[len(locals_)])
        copy.start()
        locals_.append(copy)

    pushes, gate_copies = [], []
    for d in range(1, n):
        to = lax.rem(me + d, n)
        peer = {"expert": to}
        rows = pl.ds(pl.multiple_of(g * (depth // 2), depth // 2), depth // 2)
        into = pl.ds(pl.multiple_of(me * depth + g * (depth // 2), depth // 2), depth // 2)
        a = remote(gu.at[to, rows], wd.at[into], push_s.at[3 * d], push_r.at[3 * d], peer)
        rows = pl.ds(pl.multiple_of(g * (units // 2), units // 2), units // 2)
        into = pl.ds(pl.multiple_of(owned * share + g * (units // 2), 16), units // 2)
        b = remote(
            dn.at[to, rows], w2.at[into, rows_of(me, depth)], push_s.at[3 * d + 1], push_r.at[3 * d + 1], peer
        )
        c = remote(gates.at[to], all_gates.at[me], push_s.at[3 * d + 2], push_r.at[3 * d + 2], peer)
        for copy in (c, a, b):
            copy.start()
        pushes.append((a, b))
        gate_copies.append(c)
    swaps = []

    def swap_expert(j):
        away = pl.ds(pl.multiple_of((1 - h) * share, 128), share)
        stay = pl.ds(pl.multiple_of(h * share, 128), share)
        for i, w in enumerate((eg, eu)):
            spot = w1.at[rows_of(h, width), pl.ds((2 * j + i) * share, share)]
            k = 3 * j + i
            swaps.append(remote(w.at[j, :, away], spot, exp_s.at[k], exp_r.at[k], mate))
            swaps[-1].start()
            keep(w.at[j, :, stay], spot)
        spot = w2.at[pl.ds(j * share, share), mine]
        away = pl.ds(pl.multiple_of((1 - h) * share, 16), share)
        stay = pl.ds(pl.multiple_of(h * share, 16), share)
        swaps.append(remote(ed.at[j, away], spot, exp_s.at[3 * j + 2], exp_r.at[3 * j + 2], mate))
        swaps[-1].start()
        keep(ed.at[j, stay], spot)

    for t in range(kinds):
        to_mate(t, me, 0, tokens, 0, tok.at[t])
        keep(tok.at[t], block(t, me, 0, tokens))
    keep(gu.at[me], wd.at[rows_of(me, depth)])
    keep(dn.at[me], w2.at[pl.ds(owned * share, units), rows_of(me, depth)])
    keep(gates.at[me], all_gates.at[me])

    for j in range(owned):
        swap_expert(j)
    forwards = []

    def from_mate(t, k):
        step, way = (k + 1) // 2, (k + 1) % 2
        lo, size = (0, tokens) if k == 0 else span(step, way)
        origin = ring_index(place if k == 0 else (place - step if way == 0 else place + step), n)
        theirs = pl.ds(pl.multiple_of((1 - h) * width, width), width)
        rows = pl.ds(pl.multiple_of(origin * tokens + lo, size), size)
        view = all_tok.at[t, rows, theirs]
        k = t * (n + 1) + k
        remote(view, view, core_s.at[k], core_r.at[k], mate).wait_recv()

    def swish(gate, up):
        return gate / (1.0 + jnp.exp(-gate)) * up

    def experts(first, count):
        def body(i, carry):
            origin = ring_index(place + first + i, n)
            rows = rows_of(origin, tokens)
            sums = jnp.dot(all_tok[0, rows], w1[...], preferred_element_type=jnp.float32)
            scale = all_gates[origin].T
            for j in range(owned):
                gate = sums[:, 2 * j * share : (2 * j + 1) * share]
                up = sums[:, (2 * j + 1) * share : (2 * j + 2) * share]
                value = swish(gate, up) * scale[:, j : j + 1]
                acts[rows, j * share : (j + 1) * share] = value.astype(jnp.bfloat16)
            return carry

        lax.fori_loop(0, count, body, 0)

    def dense():
        def body(i, carry):
            rows = rows_of(i, 2 * tokens)
            sums = jnp.dot(all_tok[1, rows], wd[...], preferred_element_type=jnp.float32)
            value = swish(sums[:, :units], sums[:, units:])
            acts[rows, owned * share : owned * share + units] = value.astype(jnp.bfloat16)
            return carry

        lax.fori_loop(0, n // 2, body, 0)

    def pass_on(d):
        for copy in pushes[d - 1]:
            copy.wait_recv()
        source = lax.rem(me - d + n, n)
        into = pl.ds(pl.multiple_of(source * depth + g * (depth // 2), depth // 2), depth // 2)
        a = remote(wd.at[into], wd.at[into], fwd_s.at[2 * d], fwd_r.at[2 * d], twin)
        into = pl.ds(pl.multiple_of(owned * share + g * (units // 2), 16), units // 2)
        spot = w2.at[into, rows_of(source, depth)]
        b = remote(spot, spot, fwd_s.at[2 * d + 1], fwd_r.at[2 * d + 1], twin)
        for copy in (a, b):
            copy.start()
            forwards.append(copy)

    late = list(range(1, n))
    for step in range(1, half + 1):
        for t in range(kinds):
            for way in range(2):
                hop(t, step, way).wait_recv()
                origin = ring_index(place - step if way == 0 else place + step, n)
                lo, size = span(step, way)
                if step < half:
                    start(hop(t, step + 1, way))
                to_mate(t, origin, lo, size, 2 * step - 1 + way)
        if step == half - 1:
            for _ in range(half - 1):
                pass_on(late.pop(0))
            for copy in swaps:
                copy.wait()
            for copy in locals_:
                copy.wait()
            for copy in gate_copies:
                copy.wait()
            for k in range(2 * half - 3):
                from_mate(0, k)
            experts(2 - half, 2 * half - 3)
    while late:
        pass_on(late.pop(0))
    for k in range(2 * half - 3, n + 1):
        from_mate(0, k)
    experts(half - 1, 3)
    for k in range(n + 1):
        from_mate(1, k)
    for copy in forwards:
        copy.wait()
    dense()
    for copy in pending:
        copy.wait_send()
    for group in pushes:
        for copy in group:
            copy.wait_send()


def gather(n, tok, gates, gu, dn, eg, eu, ed):
    kinds, tokens, width = tok.shape
    owned, _, hidden_units = eg.shape
    depth, units = gu.shape[1], dn.shape[1]
    share = hidden_units // 2
    dma = lambda count: pltpu.SemaphoreType.DMA((count,))
    shape = jax.ShapeDtypeStruct
    bf16 = jnp.bfloat16
    return pl.pallas_call(
        functools.partial(gather_kernel, n),
        out_shape=(
            shape((n * tokens, owned * share + units), bf16),
            shape((owned * share + units, 2 * width), bf16),
        ),
        in_specs=[pl.BlockSpec(memory_space=pl.ANY)] * 7,
        out_specs=[pl.BlockSpec(memory_space=pltpu.VMEM)] * 2,
        scratch_shapes=[
            pltpu.VMEM((kinds, n * tokens, 2 * width), bf16),
            pltpu.VMEM(gates.shape, gates.dtype),
            pltpu.VMEM((2 * width, 2 * owned * share), bf16),
            pltpu.VMEM((n * depth, gu.shape[2]), bf16),
        ]
        + [dma(kinds * n)] * 2
        + [dma(kinds * (n + 1))] * 2
        + [dma(3 * owned)] * 2
        + [dma(3 * n)] * 2
        + [dma(2 * n)] * 2
        + [dma(3 * owned + kinds + 3)],
        compiler_params=pltpu.CompilerParams(
            collective_id=0, has_side_effects=True, vmem_limit_bytes=48 * 2**20
        ),
    )(tok, gates, gu, dn, eg, eu, ed)


def reduce_kernel(n, acts, w2, out, part, core, sent, got, core_s, core_r, ring_s, ring_r):
    me, h = lax.axis_index("expert"), lax.axis_index("hidden")
    tokens, width = out.shape
    half = n // 2
    place = ring_place(me, n)
    right, left = {"expert": ring_index(place + 1, n)}, {"expert": ring_index(place - 1, n)}
    mate = {"hidden": 1 - h}
    greet([right, left, mate])
    mine = pl.ds(pl.multiple_of(h * width, width), width)
    theirs = pl.ds(pl.multiple_of((1 - h) * width, width), width)
    order = [half]
    for d in range(half - 1, 0, -1):
        order += [d, -d]
    order.append(0)
    trades = {}

    def make(d):
        k = order.index(d)
        rows = rows_of(ring_index(place + d, n), tokens)
        part[rows] = jnp.dot(acts[rows], w2[...], preferred_element_type=jnp.float32).astype(jnp.bfloat16)
        trades[d] = remote(part.at[rows, theirs], core.at[rows], core_s.at[k], core_r.at[k], mate)
        trades[d].start()

    def own(d):
        trades[d].wait_recv()
        rows = rows_of(ring_index(place + d, n), tokens)
        return part[rows, mine].astype(jnp.float32) + core[rows].astype(jnp.float32)

    def view(buffer, step, way):
        k = way * half + step - 1
        if step == 1:
            return buffer.at[k, pl.ds(way * (tokens // 2), tokens // 2)]
        return buffer.at[k]

    def hop(step, way):
        k = way * half + step - 1
        return remote(
            view(sent, step, way), view(got, step, way), ring_s.at[k], ring_r.at[k], right if way == 0 else left
        )

    make(half)
    make(half - 1)
    make(1 - half)
    far = own(half).astype(jnp.bfloat16)
    hops = []
    for step in range(1, half + 1):
        for way in range(2):
            k = way * half + step - 1
            if step == 1:
                lo = way * (tokens // 2)
                sent[k, pl.ds(lo, tokens // 2)] = far[lo : lo + tokens // 2]
            else:
                d = half + 1 - step
                value = own(d if way == 0 else -d)
                hop(step - 1, way).wait_recv()
                if step == 2:
                    lo = way * (tokens // 2)
                    other = tokens // 2 - lo
                    cut = slice(lo, lo + tokens // 2)
                    add = got[k - 1, pl.ds(lo, tokens // 2)].astype(jnp.float32)
                    sent[k, pl.ds(lo, tokens // 2)] = (value[cut] + add).astype(jnp.bfloat16)
                    sent[k, pl.ds(other, tokens // 2)] = value[other : other + tokens // 2].astype(jnp.bfloat16)
                else:
                    sent[k] = (value + got[k - 1].astype(jnp.float32)).astype(jnp.bfloat16)
            copy = hop(step, way)
            copy.start()
            hops.append(copy)
        d = half - 1 - step
        if d >= 0:
            make(d)
        if d > 0:
            make(-d)
    value = own(0)
    for way in range(2):
        hop(half, way).wait_recv()
        value = value + got[way * half + half - 1].astype(jnp.float32)
    out[...] = value.astype(jnp.bfloat16)
    for copy in hops:
        copy.wait_send()
    for copy in trades.values():
        copy.wait_send()


def reduce_sum(n, acts, w2):
    tokens, width = acts.shape[0] // n, w2.shape[1] // 2
    bf16 = jnp.bfloat16
    dma = lambda count: pltpu.SemaphoreType.DMA((count,))
    return pl.pallas_call(
        functools.partial(reduce_kernel, n),
        out_shape=jax.ShapeDtypeStruct((tokens, width), bf16),
        in_specs=[pl.BlockSpec(memory_space=pltpu.VMEM)] * 2,
        out_specs=pl.BlockSpec(memory_space=pltpu.VMEM),
        scratch_shapes=[
            pltpu.VMEM((n * tokens, 2 * width), bf16),
            pltpu.VMEM((n * tokens, width), bf16),
            pltpu.VMEM((n, tokens, width), bf16),
            pltpu.VMEM((n, tokens, width), bf16),
            dma(n), dma(n), dma(n), dma(n),
        ],
        compiler_params=pltpu.CompilerParams(
            collective_id=1, has_side_effects=True, vmem_limit_bytes=40 * 2**20
        ),
    )(acts, w2)


def kernel_fits(tokens, width, share, depth, units):
    pairs = lax.axis_size("hidden") == 2 and lax.axis_size("groups") == 2
    even = lax.axis_size("expert") % 2 == 0 and lax.axis_size("expert") >= 4
    aligned = tokens % 128 == 0 and width % 128 == 0 and share % 128 == 0
    return pairs and even and aligned and depth % 128 == 0 and units % 32 == 0


def by_kernels(routed, normed, gates, expert_gate, expert_up, expert_down, dense_gate, dense_up, dense_down):
    n = lax.axis_size("expert")
    tokens = routed.shape[0]
    owned, _, hidden_units = expert_gate.shape
    share = hidden_units // 2
    depth, spread = dense_gate.shape
    units = spread // n
    bf16 = jnp.bfloat16
    cut = lambda w: w.reshape(depth, n, units).transpose(1, 0, 2)
    gu = jnp.concatenate([cut(dense_gate), cut(dense_up)], axis=2)
    dn = dense_down.reshape(n, units, depth)
    pad = -owned % 8
    packed = jnp.pad(gates.T.reshape(n, owned, tokens), ((0, 0), (0, pad), (0, 0)))
    acts, w2 = gather(
        n, jnp.stack([routed, normed]), packed, gu, dn, expert_gate, expert_up, expert_down
    )
    return reduce_sum(n, acts, w2)


def own_gates(expert_ids, gate_values, experts_all):
    hit = expert_ids[:, :, None] == jnp.arange(experts_all, dtype=jnp.int32)[None, None, :]
    return jnp.sum(jnp.where(hit, gate_values[:, :, None], 0.0), axis=1)


def normalize(current, norm_gain):
    width = current.shape[1]
    wide = current.astype(jnp.float32)
    total = lax.psum(jnp.sum(wide * wide, axis=1, keepdims=True), "hidden")
    mean_square = total / norm_gain.shape[0]
    gain = lax.dynamic_slice_in_dim(norm_gain, lax.axis_index("hidden") * width, width)
    return (wide * gain[None, :] / jnp.sqrt(mean_square + 1e-06)).astype(jnp.bfloat16)


def swiglu(rows, gate, up):
    gate_sum = jnp.dot(rows, gate, preferred_element_type=jnp.float32)
    up_sum = jnp.dot(rows, up, preferred_element_type=jnp.float32)
    return jax.nn.silu(gate_sum) * up_sum


def local(
    current,
    previous,
    expert_ids,
    gate_values,
    norm_gain,
    expert_gate,
    expert_up,
    expert_down,
    dense_gate,
    dense_up,
    dense_down,
):
    owned = expert_gate.shape[0]
    owners = lax.axis_size("expert")
    bf16 = jnp.bfloat16
    routed = previous.astype(bf16)
    normed = normalize(current, norm_gain)
    gates = own_gates(expert_ids, gate_values, owned * owners)
    share, units = expert_gate.shape[2] // 2, dense_gate.shape[1] // owners
    if kernel_fits(*routed.shape, share, dense_gate.shape[0], units):
        return by_kernels(
            routed, normed, gates, expert_gate, expert_up, expert_down, dense_gate, dense_up, dense_down
        )
    swap = lambda w, axis, cut, join: lax.all_to_all(w, axis, split_axis=cut, concat_axis=join, tiled=True)
    wg = swap(expert_gate, "hidden", 2, 1)
    wu = swap(expert_up, "hidden", 2, 1)
    wd = swap(expert_down, "hidden", 1, 2)
    both = lax.all_gather(jnp.stack([routed, normed]), "expert", axis=1, tiled=True)
    both = lax.all_gather(both, "hidden", axis=2, tiled=True)
    mine = swap(gates, "expert", 1, 0)
    dg = swap(dense_gate, "expert", 1, 0)
    du = swap(dense_up, "expert", 1, 0)
    dd = swap(dense_down, "expert", 0, 1)
    acts = [
        (swiglu(both[0], wg[j], wu[j]) * mine[:, j : j + 1]).astype(bf16) for j in range(owned)
    ]
    acts.append(swiglu(both[1], dg, du).astype(bf16))
    downs = [wd[j] for j in range(owned)] + [dd]
    total = jnp.dot(
        jnp.concatenate(acts, axis=1), jnp.concatenate(downs, axis=0), preferred_element_type=jnp.float32
    ).astype(bf16)
    half = lax.psum_scatter(total, "hidden", scatter_dimension=1, tiled=True)
    return lax.psum_scatter(half, "expert", scatter_dimension=0, tiled=True)


def solution(mesh):
    placed = (
        P(("groups", "expert"), "hidden"),
        P(("groups", "expert"), "hidden"),
        P(("groups", "expert"), None),
        P(("groups", "expert"), None),
        P(),
        P("expert", "hidden", None),
        P("expert", "hidden", None),
        P("expert", None, "hidden"),
        P("expert", "hidden"),
        P("expert", "hidden"),
        P("hidden", "expert"),
    )
    return jax.shard_map(
        local,
        mesh=mesh,
        in_specs=placed,
        out_specs=P(("groups", "expert"), "hidden"),
        check_vma=False,
    )
```
